512 devices in a mesh: inst: 2 (over y_hi), blk: 256 (over z, y_lo, x, core).
Axes of the slice: x: 4, y: 8 (y_hi: 2, y_lo: 4; y = y_hi * 4 + y_lo), z: 8, core: 2. Of those that a mesh axis runs over, the one named last changes fastest.
Arguments:
- state: float32 [8, 5, 256, 32, 256], P('inst', None, 'blk'), as said below
- slot_of: int32 [256], replicated, may hold values from 0 to 255, as said below
- conn_block: int32 [256, 2], replicated, may hold values from 0 to 255, as said below
- conn_side: int32 [256, 2], replicated, may hold values from 0 to 1
- conn_shift: int32 [256, 2], replicated, may hold values from 0 to 255
- rows: int32 [256], replicated, may hold values from 16 to 32
Outputs:
- residual: float32 [8, 5, 256, 32, 256], P('inst', None, 'blk')
The draws below stay inside these ranges and needn't reach their ends.
Inputs may be any that keep to these rules, and one draw needn't show every extreme that they name: slot_of is a permutation of the block numbers. With d(b) = slot_of[b], the index along blk of the device holding block b, d(conn_block[b, f]) - d(b) taken cyclically modulo the number of blk devices lies within -2 to 2; both ends are reached in every draw. `state`: density and pressure are positive.
All inputs are finite; a program needn't handle non-finite values.
Results may differ from the reference program's by a relative error of at most 0.00012.
Values sent between devices are 32-bit elements; how exact they have to be, the bound alone decides.
A program may use at most 64 MiB of HBM per device.

```python
import math
import jax
import jax.numpy as jnp
from jax import lax

INSTANCES = 8
REACH = 2
BLK_DEV = 1
NI = 32
NJ = 256
BLOCKS = 256


def draw_state(key, part):
    key_density, key_momentum, key_pressure = jax.random.split(key, 3)
    shape = (INSTANCES, BLOCKS, NI, NJ)
    density = jnp.exp(jax.random.uniform(key_density, shape, jnp.float32, -0.5, 0.45))
    momentum = jnp.clip(0.4 * jax.random.normal(key_momentum, (3,) + shape, jnp.float32), -1.5, 1.5)
    pressure = jax.random.uniform(key_pressure, shape, jnp.float32, 0.6, 1.4)
    energy = pressure / 0.4 + 0.5 * (momentum[0] * momentum[0] + momentum[1] * momentum[1] + momentum[2] * momentum[2]) / density
    return jnp.stack([density, momentum[0], momentum[1], momentum[2], energy], axis=1).astype(jnp.float32)


def block_slots(key):
    return jax.random.permutation(jax.random.fold_in(key, 11), BLOCKS).astype(jnp.int32)


def draw_slot_of(key, part):
    return block_slots(key)


def draw_conn_block(key, part):
    slot_of = block_slots(key)
    ids_of_slot = jnp.zeros((BLOCKS,), jnp.int32).at[slot_of].set(jnp.arange(BLOCKS, dtype=jnp.int32))
    delta = jax.random.randint(jax.random.fold_in(key, 12), (BLOCKS, 2), -REACH, REACH + 1).astype(jnp.int32)
    first = (jnp.arange(BLOCKS, dtype=jnp.int32) == ids_of_slot[0])[:, None]
    forced = jnp.array([[-REACH, REACH]], jnp.int32)
    delta = jnp.where(first, forced, delta)
    within = jax.random.randint(jax.random.fold_in(key, 13), (BLOCKS, 2), 0, BLK_DEV).astype(jnp.int32)
    span = BLOCKS // BLK_DEV
    home = (slot_of // BLK_DEV)[:, None]
    target = jnp.mod(home + delta, span) * BLK_DEV + within
    return ids_of_slot[target].astype(jnp.int32)


def set_ends(entries, stream_key, smallest, top_value):
    place = [jax.random.randint(jax.random.fold_in(stream_key, axis), (), 0, length) for axis, length in enumerate(entries.shape)]
    main_axis = entries.shape.index(max(entries.shape))
    neighbour = place[:main_axis] + [(place[main_axis] + 1) % entries.shape[main_axis]] + place[main_axis + 1:]
    return entries.at[tuple(place)].set(smallest).at[tuple(neighbour)].set(top_value)


def setup_inputs(seed: int = 0) -> dict:
    splits = jax.random.split(jax.random.key(seed), 7)
    return {
        "state": draw_state(jax.random.fold_in(splits[6], 71), 0),
        "slot_of": draw_slot_of(jax.random.fold_in(splits[6], 71), 0),
        "conn_block": draw_conn_block(jax.random.fold_in(splits[6], 71), 0),
        "conn_side": set_ends(jax.random.randint(splits[3], (BLOCKS, 2), 0, 2), jax.random.fold_in(splits[3], 1), 0, 1).astype(jnp.int32),
        "conn_shift": set_ends(jax.random.randint(splits[4], (BLOCKS, 2), 0, NJ), jax.random.fold_in(splits[4], 1), 0, NJ - 1).astype(jnp.int32),
        "rows": set_ends(jax.random.randint(splits[5], (BLOCKS,), NI // 2, NI + 1), jax.random.fold_in(splits[5], 1), NI // 2, NI).astype(jnp.int32),
    }


GAMMA_MINUS = 0.4
DAMPING = 0.05
FREQUENCY = 1.0


def spectral_matrix(count):
    position = jnp.arange(count, dtype=jnp.int32)
    offset = position[:, None] - position[None, :]
    angle = (math.pi / count) * offset.astype(jnp.float32)
    safe_sin = jnp.where(offset == 0, 1.0, jnp.sin(angle))
    parity = 1.0 - 2.0 * jnp.mod(offset, 2).astype(jnp.float32)
    return jnp.where(offset == 0, 0.0, 0.5 * FREQUENCY * parity * jnp.cos(angle) / safe_sin).astype(jnp.float32)


def euler_flux(fields, direction):
    density = fields[:, 0]
    momentum_x = fields[:, 1]
    momentum_y = fields[:, 2]
    momentum_z = fields[:, 3]
    energy = fields[:, 4]
    pressure = GAMMA_MINUS * (energy - 0.5 * (momentum_x * momentum_x + momentum_y * momentum_y + momentum_z * momentum_z) / density)
    velocity = fields[:, direction] / density
    parts = [fields[:, direction], momentum_x * velocity, momentum_y * velocity, momentum_z * velocity, (energy + pressure) * velocity]
    parts[direction] = parts[direction] + pressure
    return jnp.stack(parts, axis=1)


def face_rims(fields, block_rows):
    layers = jnp.arange(2, dtype=jnp.int32)
    low_rows = jnp.broadcast_to(layers[None, :], (block_rows.shape[0], 2))
    high_rows = block_rows[:, None] - 1 - layers[None, :]
    row_index = jnp.concatenate([low_rows, high_rows], axis=1)
    shape = fields.shape[:3] + (4, fields.shape[4])
    full_index = jnp.broadcast_to(row_index[None, None, :, :, None], shape)
    boundary = jnp.take_along_axis(fields, full_index, axis=3)
    return boundary.reshape(fields.shape[:3] + (2, 2, fields.shape[4]))


def face_ghosts(all_rims, nb_slots, nb_side, shift):
    picked = all_rims[:, :, nb_slots, nb_side]
    count = all_rims.shape[-1]
    columns = jnp.mod(jnp.arange(count, dtype=jnp.int32)[None, None, :] + shift[:, :, None], count)
    columns = jnp.broadcast_to(columns[None, None, :, :, None, :], picked.shape)
    return jnp.take_along_axis(picked, columns, axis=5)


def spatial_residual(fields, ghosts, block_rows):
    row_count = fields.shape[3]
    stacked = jnp.concatenate([ghosts[:, :, :, 0, ::-1], fields, ghosts[:, :, :, 1]], axis=3)
    position = jnp.arange(row_count + 4, dtype=jnp.int32)
    beyond = position[None, :] - 2 - block_rows[:, None]
    source_row = jnp.where(beyond < 0, position[None, :], row_count + 2 + jnp.minimum(beyond, 1))
    source_row = jnp.broadcast_to(source_row[None, None, :, :, None], stacked.shape)
    extended = jnp.take_along_axis(stacked, source_row, axis=3)
    flux_rows = euler_flux(extended, 1)
    slope_rows = (8.0 * (flux_rows[:, :, :, 3:-1] - flux_rows[:, :, :, 1:-3]) - (flux_rows[:, :, :, 4:] - flux_rows[:, :, :, :-4])) / 12.0
    smooth_rows = extended[:, :, :, 4:] - 4.0 * extended[:, :, :, 3:-1] + 6.0 * extended[:, :, :, 2:-2] - 4.0 * extended[:, :, :, 1:-3] + extended[:, :, :, :-4]
    flux_cols = euler_flux(fields, 2)
    slope_cols = (8.0 * (jnp.roll(flux_cols, -1, 4) - jnp.roll(flux_cols, 1, 4)) - (jnp.roll(flux_cols, -2, 4) - jnp.roll(flux_cols, 2, 4))) / 12.0
    smooth_cols = jnp.roll(fields, -2, 4) - 4.0 * jnp.roll(fields, -1, 4) + 6.0 * fields - 4.0 * jnp.roll(fields, 1, 4) + jnp.roll(fields, 2, 4)
    return -(slope_rows + slope_cols) - DAMPING * (smooth_rows + smooth_cols)


def reference(state, slot_of, conn_block, conn_side, conn_shift, rows):
    blocks = slot_of.shape[0]
    ids_of_slot = jnp.zeros((blocks,), jnp.int32).at[slot_of].set(jnp.arange(blocks, dtype=jnp.int32))
    slot_rows = rows[ids_of_slot]
    nb_slots = slot_of[conn_block[ids_of_slot]]
    nb_side = conn_side[ids_of_slot]
    shift = conn_shift[ids_of_slot]
    inside = (jnp.arange(NI, dtype=jnp.int32)[None, :] < slot_rows[:, None])[None, None, :, :, None]

    def one_instance(fields):
        fields = fields[None]
        boundary = face_rims(fields, slot_rows)
        ghosts = face_ghosts(boundary, nb_slots, nb_side, shift)
        return spatial_residual(fields, ghosts, slot_rows)[0]

    spatial = lax.map(one_instance, state)
    source = jnp.einsum("nm,mvbij->nvbij", spectral_matrix(INSTANCES), state, precision=lax.Precision.HIGHEST)
    return jnp.where(inside, spatial - source, 0.0).astype(jnp.float32)
```

```python
import functools
import math

import jax
import jax.numpy as jnp
from jax import lax
from jax.experimental import pallas as pl
from jax.experimental.pallas import tpu as pltpu
from jax.sharding import PartitionSpec as P

REACH = 2
GAMMA_MINUS = 0.4
DAMPING = 0.05
FREQUENCY = 1.0
MESH = pl.DeviceIdType.MESH
STEPS = [step for step in range(-REACH, REACH + 1) if step != 0]
EARLY = 2


def spectral_weight(offset, count):
    offset %= count
    if offset == 0 or 2 * offset == count:
        return 0.0
    return 0.5 * FREQUENCY * (-1.0) ** offset / math.tan(math.pi * offset / count)


def weighted_sum(weights, values):
    total = None
    for weight, value in zip(weights, values):
        if weight == 0.0:
            continue
        term = weight * value
        total = term if total is None else total + term
    return total


def differences(flux, fields, axis):
    size = fields.shape[axis]
    wide = flux * (8.0 / 12.0)
    narrow = flux * (1.0 / 12.0)
    near = fields * (4.0 * DAMPING)
    far = fields * DAMPING
    ahead = (near - wide) + pltpu.roll(narrow - far, size - 1, axis)
    behind = (near + wide) - pltpu.roll(narrow + far, 1, axis)
    return (
        pltpu.roll(ahead, size - 1, axis)
        + pltpu.roll(behind, 1, axis)
        - fields * (6.0 * DAMPING)
    )


def flux_parts(fields, pressure, inverse, direction):
    velocity = fields[direction] * inverse
    parts = [
        fields[direction],
        fields[1] * velocity,
        fields[2] * velocity,
        fields[3] * velocity,
        (fields[4] + pressure) * velocity,
    ]
    parts[direction] = parts[direction] + pressure
    return parts


def kernel(
    instances, x_hbm, slot_hbm, block_hbm, side_hbm, shift_hbm, rows_hbm, out,
    near, far, rims, ghosts, slot, block, side, shift, rows,
    in_sems, far_send, far_recv, rim_send, rim_recv,
):
    here, count_v, row_count, columns = near.shape
    inst = lax.axis_index("inst")
    me = lax.axis_index("blk")
    span = lax.axis_size("blk")
    partner = (1 - inst, me)

    local = [
        pltpu.make_async_copy(source, target, in_sems.at[place])
        for place, (source, target) in enumerate(
            [
                (slot_hbm, slot),
                (rows_hbm, rows),
                (block_hbm, block),
                (side_hbm, side),
                (shift_hbm, shift),
                (x_hbm, near),
            ]
        )
    ]
    for copy in local:
        copy.start()

    barrier = pltpu.get_barrier_semaphore()
    pl.semaphore_signal(barrier, inc=1, device_id=partner, device_id_type=MESH)
    for step in STEPS:
        pl.semaphore_signal(
            barrier,
            inc=1,
            device_id=(inst, lax.rem(me + step + span, span)),
            device_id_type=MESH,
        )
    pl.semaphore_wait(barrier, 1 + len(STEPS))

    far_copies = [
        pltpu.make_async_remote_copy(
            src_ref=x_hbm.at[:, v],
            dst_ref=far.at[:, v],
            send_sem=far_send.at[v],
            recv_sem=far_recv.at[v],
            device_id=partner,
            device_id_type=MESH,
        )
        for v in range(count_v)
    ]
    for copy in far_copies[:EARLY]:
        copy.start()

    for copy in local:
        copy.wait()
    slots = slot[...]
    numbers = lax.broadcasted_iota(jnp.int32, slots.shape, 1)
    mine = slots == me

    def looked_up(mask, values):
        return jnp.sum(jnp.where(mask, values, 0))

    my_rows = looked_up(mine, rows[...])
    picks = []
    shifts = []
    for face in range(2):
        neighbour = looked_up(mine, block[face : face + 1, :])
        neighbour_slot = looked_up(numbers == neighbour, slots)
        distance = lax.rem(neighbour_slot - me + (REACH + span), span)
        picks.append(
            jnp.clip(
                2 * distance + looked_up(mine, side[face : face + 1, :]), 0, rims.shape[0] - 1
            )
        )
        shifts.append(looked_up(mine, shift[face : face + 1, :]))

    high = [jnp.clip(my_rows - 1 - layer, 0, row_count - 1) for layer in range(2)]

    def gather_rim(v, carry):
        for n in range(here):
            rims[2 * REACH, v, 2 * n : 2 * n + 2, :] = near[n, v, 0:2, :]
            for layer in range(2):
                rims[2 * REACH + 1, v, 2 * n + layer : 2 * n + layer + 1, :] = near[
                    n, v, pl.ds(high[layer], 1), :
                ]
        return carry

    lax.fori_loop(0, count_v, gather_rim, 0)

    rim_copies = [
        pltpu.make_async_remote_copy(
            src_ref=rims.at[2 * REACH : 2 * REACH + 2],
            dst_ref=rims.at[2 * (REACH - step) : 2 * (REACH - step) + 2],
            send_sem=rim_send.at[REACH - step],
            recv_sem=rim_recv.at[REACH - step],
            device_id=(inst, lax.rem(me + step + span, span)),
            device_id_type=MESH,
        )
        for step in STEPS
    ]
    for copy in rim_copies:
        copy.start()
    for copy in far_copies[EARLY:]:
        copy.start()

    def own_source(v, carry):
        values = [near[m, v] for m in range(here)]
        for n in range(here):
            out[n, v] = weighted_sum(
                [-spectral_weight(n - m, instances) for m in range(here)], values
            )
        return carry

    lax.fori_loop(0, count_v, own_source, 0)

    for copy in rim_copies:
        copy.wait_recv()
    for face in range(2):
        picked = rims[picks[face]]
        amount = columns - shifts[face]
        for v in range(count_v):
            ghosts[face, v] = pltpu.roll(picked[v], amount, 1)

    extent = row_count + 8
    position = lax.broadcasted_iota(jnp.int32, (extent, columns), 0)
    first_beyond = position == my_rows
    second_beyond = position == my_rows + 1
    last_row = lax.broadcasted_iota(jnp.int32, (8, columns), 0) == 7

    def spatial(n, carry):
        fields = []
        for v in range(count_v):
            low = [ghosts[0, v, pl.ds(2 * n + layer, 1), :] for layer in range(2)]
            top = [ghosts[1, v, pl.ds(2 * n + layer, 1), :] for layer in range(2)]
            before = jnp.where(last_row, low[0], low[1])
            block_rows = jnp.concatenate([near[n, v], before], axis=0)
            fields.append(
                jnp.where(first_beyond, top[0], jnp.where(second_beyond, top[1], block_rows))
            )
        inverse = 1.0 / fields[0]
        squares = fields[1] * fields[1] + fields[2] * fields[2] + fields[3] * fields[3]
        pressure = GAMMA_MINUS * (fields[4] - 0.5 * squares * inverse)
        for v, flux in enumerate(flux_parts(fields, pressure, inverse, 1)):
            out[n, v] += differences(flux, fields[v], 0)[:row_count]
        fields = [field[:row_count] for field in fields]
        pressure = pressure[:row_count]
        inverse = inverse[:row_count]
        for v, flux in enumerate(flux_parts(fields, pressure, inverse, 2)):
            out[n, v] += differences(flux, fields[v], 1)
        return carry

    lax.fori_loop(0, here, spatial, 0)

    inside = lax.broadcasted_iota(jnp.int32, (row_count, columns), 0) < my_rows
    for v in range(count_v):
        far_copies[v].wait_recv()
        values = [far[m, v] for m in range(here)]
        for n in range(here):
            source = weighted_sum(
                [spectral_weight(n - m - here, instances) for m in range(here)], values
            )
            out[n, v] = jnp.where(inside, out[n, v] - source, 0.0)
    for copy in far_copies + rim_copies:
        copy.wait_send()


def on_device(state, slot_of, conn_block, conn_side, conn_shift, rows):
    here, count_v, _, row_count, columns = state.shape
    instances = here * lax.axis_size("inst")
    blocks = slot_of.shape[0]
    whole = (here, count_v, row_count, columns)
    result = pl.pallas_call(
        functools.partial(kernel, instances),
        out_shape=jax.ShapeDtypeStruct(whole, jnp.float32),
        in_specs=[pl.BlockSpec(memory_space=pl.ANY)] * 6,
        out_specs=pl.BlockSpec(memory_space=pltpu.VMEM),
        scratch_shapes=[
            pltpu.VMEM(whole, jnp.float32),
            pltpu.VMEM(whole, jnp.float32),
            pltpu.VMEM((2 * (2 * REACH + 1), count_v, 2 * here, columns), jnp.float32),
            pltpu.VMEM((2, count_v, 2 * here, columns), jnp.float32),
            pltpu.VMEM((1, blocks), jnp.int32),
            pltpu.VMEM((2, blocks), jnp.int32),
            pltpu.VMEM((2, blocks), jnp.int32),
            pltpu.VMEM((2, blocks), jnp.int32),
            pltpu.VMEM((1, blocks), jnp.int32),
            pltpu.SemaphoreType.DMA((6,)),
            pltpu.SemaphoreType.DMA((count_v,)),
            pltpu.SemaphoreType.DMA((count_v,)),
            pltpu.SemaphoreType.DMA((2 * REACH + 1,)),
            pltpu.SemaphoreType.DMA((2 * REACH + 1,)),
        ],
        compiler_params=pltpu.CompilerParams(collective_id=0, has_side_effects=True),
        name="residual",
    )(
        state.reshape(whole),
        slot_of.reshape(1, blocks),
        conn_block.T,
        conn_side.T,
        conn_shift.T,
        rows.reshape(1, blocks),
    )
    return result.reshape(state.shape)


def solution(mesh):
    in_specs = (P("inst", None, "blk", None, None), P(), P(), P(), P(), P())
    out_specs = P("inst", None, "blk", None, None)
    return jax.shard_map(
        on_device, mesh=mesh, in_specs=in_specs, out_specs=out_specs, check_vma=False
    )
```

```python
import functools
import math

import jax
import jax.numpy as jnp
from jax import lax
from jax.experimental import pallas as pl
from jax.experimental.pallas import tpu as pltpu
from jax.sharding import PartitionSpec as P

REACH = 2
GAMMA_MINUS = 0.4
DAMPING = 0.05
FREQUENCY = 1.0
MESH = pl.DeviceIdType.MESH
OWN = REACH
STEPS = (-2, 2, -1, 1)
BATCHES = (4, 12)


def spectral_weight(offset, count):
    offset %= count
    if offset == 0 or 2 * offset == count:
        return 0.0
    return 0.5 * FREQUENCY * (-1.0) ** offset / math.tan(math.pi * offset / count)


def weighted_sum(weights, values):
    total = None
    for weight, value in zip(weights, values):
        if weight == 0.0:
            continue
        term = weight * value
        total = term if total is None else total + term
    return total


def differences(flux, fields, axis):
    size = fields.shape[axis]
    wide = flux * (8.0 / 12.0)
    narrow = flux * (1.0 / 12.0)
    near = fields * (4.0 * DAMPING)
    far = fields * DAMPING
    ahead = (near - wide) + pltpu.roll(narrow - far, size - 1, axis)
    behind = (near + wide) - pltpu.roll(narrow + far, 1, axis)
    return (
        pltpu.roll(ahead, size - 1, axis)
        + pltpu.roll(behind, 1, axis)
        - fields * (6.0 * DAMPING)
    )


def flux_parts(fields, pressure, inverse, direction):
    velocity = fields[direction] * inverse
    parts = [
        fields[direction],
        fields[1] * velocity,
        fields[2] * velocity,
        fields[3] * velocity,
        (fields[4] + pressure) * velocity,
    ]
    parts[direction] = parts[direction] + pressure
    return parts


def kernel(
    instances, x_hbm, slot_hbm, block_hbm, side_hbm, shift_hbm, rows_hbm, out,
    near, far, rims, ghosts, slot, block, side, shift, rows,
    in_sems, far_send, far_recv, rim_send, rim_recv, hop, hop_sems,
):
    here, count_v, row_count, columns = near.shape
    inst = lax.axis_index("inst")
    me = lax.axis_index("blk")
    span = lax.axis_size("blk")
    partner = (1 - inst, me)
    place = lax.rem(me // 2, 4)

    def at(step):
        return (inst, lax.rem(me + step + span, span))

    ends = (place == 0) | (place == 3)
    aside = 2 - 4 * lax.rem(place, 2)
    beside = lax.rem(me + aside + span, span)

    barrier = pltpu.get_barrier_semaphore()
    peers = [partner, (1 - inst, beside)] + [at(step) for step in STEPS]
    for device in peers:
        pl.semaphore_signal(barrier, inc=1, device_id=device, device_id_type=MESH)

    local = [
        pltpu.make_async_copy(source, target, in_sems.at[index])
        for index, (source, target) in enumerate(
            [
                (slot_hbm, slot),
                (rows_hbm, rows),
                (block_hbm, block),
                (side_hbm, side),
                (shift_hbm, shift),
                (x_hbm, near),
            ]
        )
    ]
    for copy in local:
        copy.start()

    pl.semaphore_wait(barrier, len(peers))

    far_copies = [
        pltpu.make_async_remote_copy(
            src_ref=x_hbm.at[m, v],
            dst_ref=far.at[m, v],
            send_sem=far_send.at[m, v],
            recv_sem=far_recv.at[m, v],
            device_id=partner,
            device_id_type=MESH,
        )
        for v in range(count_v)
        for m in range(here)
    ]
    moved = far_copies.pop()
    aside_copy = pltpu.make_async_remote_copy(
        src_ref=x_hbm.at[here - 1, count_v - 1],
        dst_ref=hop,
        send_sem=hop_sems.at[0],
        recv_sem=hop_sems.at[1],
        device_id=(inst, beside),
        device_id_type=MESH,
    )
    onward_copy = pltpu.make_async_remote_copy(
        src_ref=hop,
        dst_ref=far.at[here - 1, count_v - 1],
        send_sem=hop_sems.at[2],
        recv_sem=far_recv.at[here - 1, count_v - 1],
        device_id=(1 - inst, beside),
        device_id_type=MESH,
    )
    started = [0, BATCHES[0], sum(BATCHES), len(far_copies)]

    def start_far(batch):
        for copy in far_copies[started[batch] : started[batch + 1]]:
            copy.start()

    start_far(0)

    for copy in local:
        copy.wait()
    slots = slot[...]
    numbers = lax.broadcasted_iota(jnp.int32, slots.shape, 1)
    mine = slots == me

    def looked_up(mask, values):
        return jnp.sum(jnp.where(mask, values, 0))

    my_rows = looked_up(mine, rows[...])
    picks = []
    shifts = []
    for face in range(2):
        neighbour = looked_up(mine, block[face : face + 1, :])
        neighbour_slot = looked_up(numbers == neighbour, slots)
        distance = lax.rem(neighbour_slot - me + (REACH + span), span)
        picks.append(
            jnp.clip(
                2 * distance + looked_up(mine, side[face : face + 1, :]), 0, rims.shape[0] - 1
            )
        )
        shifts.append(looked_up(mine, shift[face : face + 1, :]))

    high = [jnp.clip(my_rows - 1 - layer, 0, row_count - 1) for layer in range(2)]

    def gather_rim(v, carry):
        for n in range(here):
            rims[2 * OWN, v, 2 * n : 2 * n + 2, :] = near[n, v, 0:2, :]
            for layer in range(2):
                rims[2 * OWN + 1, v, 2 * n + layer : 2 * n + layer + 1, :] = near[
                    n, v, pl.ds(high[layer], 1), :
                ]
        return carry

    lax.fori_loop(0, count_v, gather_rim, 0)

    rim_copies = [
        pltpu.make_async_remote_copy(
            src_ref=rims.at[2 * OWN : 2 * OWN + 2],
            dst_ref=rims.at[2 * (OWN - step) : 2 * (OWN - step) + 2],
            send_sem=rim_send.at[OWN - step],
            recv_sem=rim_recv.at[OWN - step],
            device_id=at(step),
            device_id_type=MESH,
        )
        for step in STEPS
    ]
    for copy in rim_copies:
        copy.start()
    pl.when(ends)(aside_copy.start)
    start_far(1)

    def own_source(v, carry):
        values = [near[m, v] for m in range(here)]
        for n in range(here):
            out[n, v] = weighted_sum(
                [-spectral_weight(n - m, instances) for m in range(here)], values
            )
        return carry

    lax.fori_loop(0, count_v, own_source, 0)

    @pl.when(jnp.logical_not(ends))
    def _():
        aside_copy.wait_recv()
        onward_copy.start()
        moved.start()

    start_far(2)
    for copy in rim_copies:
        copy.wait_recv()
    for face in range(2):
        picked = rims[picks[face]]
        amount = columns - shifts[face]
        for v in range(count_v):
            ghosts[face, v] = pltpu.roll(picked[v], amount, 1)

    extent = row_count + 8
    position = lax.broadcasted_iota(jnp.int32, (extent, columns), 0)
    first_beyond = position == my_rows
    second_beyond = position == my_rows + 1
    last_row = lax.broadcasted_iota(jnp.int32, (8, columns), 0) == 7

    def spatial(n, carry):
        fields = []
        for v in range(count_v):
            low = [ghosts[0, v, pl.ds(2 * n + layer, 1), :] for layer in range(2)]
            top = [ghosts[1, v, pl.ds(2 * n + layer, 1), :] for layer in range(2)]
            before = jnp.where(last_row, low[0], low[1])
            block_rows = jnp.concatenate([near[n, v], before], axis=0)
            fields.append(
                jnp.where(first_beyond, top[0], jnp.where(second_beyond, top[1], block_rows))
            )
        inverse = 1.0 / fields[0]
        squares = fields[1] * fields[1] + fields[2] * fields[2] + fields[3] * fields[3]
        pressure = GAMMA_MINUS * (fields[4] - 0.5 * squares * inverse)
        for v, flux in enumerate(flux_parts(fields, pressure, inverse, 1)):
            out[n, v] += differences(flux, fields[v], 0)[:row_count]
        fields = [field[:row_count] for field in fields]
        pressure = pressure[:row_count]
        inverse = inverse[:row_count]
        for v, flux in enumerate(flux_parts(fields, pressure, inverse, 2)):
            out[n, v] += differences(flux, fields[v], 1)
        return carry

    lax.fori_loop(0, here, spatial, 0)

    inside = lax.broadcasted_iota(jnp.int32, (row_count, columns), 0) < my_rows
    for v in range(count_v):
        for copy in (far_copies + [moved])[v * here : (v + 1) * here]:
            copy.wait_recv()
        values = [far[m, v] for m in range(here)]
        for n in range(here):
            source = weighted_sum(
                [spectral_weight(n - m - here, instances) for m in range(here)], values
            )
            out[n, v] = jnp.where(inside, out[n, v] - source, 0.0)
    for copy in far_copies + rim_copies:
        copy.wait_send()
    pl.when(ends)(aside_copy.wait_send)

    @pl.when(jnp.logical_not(ends))
    def _():
        onward_copy.wait_send()
        moved.wait_send()


def on_device(state, slot_of, conn_block, conn_side, conn_shift, rows):
    here, count_v, _, row_count, columns = state.shape
    instances = here * lax.axis_size("inst")
    blocks = slot_of.shape[0]
    whole = (here, count_v, row_count, columns)
    result = pl.pallas_call(
        functools.partial(kernel, instances),
        out_shape=jax.ShapeDtypeStruct(whole, jnp.float32),
        in_specs=[pl.BlockSpec(memory_space=pl.ANY)] * 6,
        out_specs=pl.BlockSpec(memory_space=pltpu.VMEM),
        scratch_shapes=[
            pltpu.VMEM(whole, jnp.float32),
            pltpu.VMEM(whole, jnp.float32),
            pltpu.VMEM((2 * (2 * REACH + 1), count_v, 2 * here, columns), jnp.float32),
            pltpu.VMEM((2, count_v, 2 * here, columns), jnp.float32),
            pltpu.VMEM((1, blocks), jnp.int32),
            pltpu.VMEM((2, blocks), jnp.int32),
            pltpu.VMEM((2, blocks), jnp.int32),
            pltpu.VMEM((2, blocks), jnp.int32),
            pltpu.VMEM((1, blocks), jnp.int32),
            pltpu.SemaphoreType.DMA((6,)),
            pltpu.SemaphoreType.DMA((here, count_v)),
            pltpu.SemaphoreType.DMA((here, count_v)),
            pltpu.SemaphoreType.DMA((2 * REACH + 1,)),
            pltpu.SemaphoreType.DMA((2 * REACH + 1,)),
            pltpu.VMEM((row_count, columns), jnp.float32),
            pltpu.SemaphoreType.DMA((3,)),
        ],
        compiler_params=pltpu.CompilerParams(
            collective_id=0, has_side_effects=True, vmem_limit_bytes=16 * 2**20
        ),
        name="residual",
    )(
        *[
            pltpu.with_memory_space_constraint(operand, pltpu.HBM)
            for operand in (
                state.reshape(whole),
                slot_of.reshape(1, blocks),
                conn_block.T,
                conn_side.T,
                conn_shift.T,
                rows.reshape(1, blocks),
            )
        ]
    )
    return result.reshape(state.shape)


def solution(mesh):
    in_specs = (P("inst", None, "blk", None, None), P(), P(), P(), P(), P())
    out_specs = P("inst", None, "blk", None, None)
    return jax.shard_map(
        on_device, mesh=mesh, in_specs=in_specs, out_specs=out_specs, check_vma=False
    )
```

```python
import functools
import math

import jax
import jax.numpy as jnp
from jax import lax
from jax.experimental import pallas as pl
from jax.experimental.pallas import tpu as pltpu
from jax.sharding import PartitionSpec as P

REACH = 2
GAMMA_MINUS = 0.4
DAMPING = 0.05
FREQUENCY = 1.0
MESH = pl.DeviceIdType.MESH
OWN = REACH
STEPS = (-2, 2, -1, 1)
BATCHES = (4, 12)


def spectral_weight(offset, count):
    offset %= count
    if offset == 0 or 2 * offset == count:
        return 0.0
    return 0.5 * FREQUENCY * (-1.0) ** offset / math.tan(math.pi * offset / count)


def weighted_sum(weights, values):
    total = None
    for weight, value in zip(weights, values):
        if weight == 0.0:
            continue
        term = weight * value
        total = term if total is None else total + term
    return total


def differences(flux, fields, axis):
    size = fields.shape[axis]
    wide = flux * (8.0 / 12.0)
    narrow = flux * (1.0 / 12.0)
    near = fields * (4.0 * DAMPING)
    far = fields * DAMPING
    ahead = (near - wide) + pltpu.roll(narrow - far, size - 1, axis)
    behind = (near + wide) - pltpu.roll(narrow + far, 1, axis)
    return (
        pltpu.roll(ahead, size - 1, axis)
        + pltpu.roll(behind, 1, axis)
        - fields * (6.0 * DAMPING)
    )


def flux_parts(fields, pressure, inverse, direction):
    velocity = fields[direction] * inverse
    parts = [
        fields[direction],
        fields[1] * velocity,
        fields[2] * velocity,
        fields[3] * velocity,
        (fields[4] + pressure) * velocity,
    ]
    parts[direction] = parts[direction] + pressure
    return parts


def kernel(
    instances, x_hbm, slot_hbm, block_hbm, side_hbm, shift_hbm, rows_hbm, out,
    near, far, rims, ghosts, slot, block, side, shift, rows,
    in_sems, far_send, far_recv, rim_send, rim_recv, hop, hop_sems, ack, cross,
):
    here, count_v, row_count, columns = near.shape
    inst = lax.axis_index("inst")
    me = lax.axis_index("blk")
    span = lax.axis_size("blk")
    partner = (1 - inst, me)
    place = lax.rem(me // 2, 4)

    def at(step):
        return (inst, lax.rem(me + step + span, span))

    ends = (place == 0) | (place == 3)
    aside = 2 - 4 * lax.rem(place, 2)
    beside = lax.rem(me + aside + span, span)

    def signal(semaphore, device):
        pl.semaphore_signal(semaphore, inc=1, device_id=device, device_id_type=MESH)

    below = {step: lax.rem(me + step + span, span) < me for step in STEPS}
    above = {step: lax.rem(me + step + span, span) > me for step in STEPS}
    barrier = pltpu.get_barrier_semaphore()
    signal(barrier, partner)
    for step in STEPS:
        pl.when(above[step])(functools.partial(signal, barrier, at(step)))
    pl.when(inst == 0)(functools.partial(signal, barrier, (1 - inst, beside)))
    greetings = 1 + inst
    for step in STEPS:
        greetings = greetings + jnp.where(below[step], 1, 0)

    local = [
        pltpu.make_async_copy(source, target, in_sems.at[index])
        for index, (source, target) in enumerate(
            [
                (slot_hbm, slot),
                (rows_hbm, rows),
                (block_hbm, block),
                (side_hbm, side),
                (shift_hbm, shift),
                (x_hbm, near),
            ]
        )
    ]
    for copy in local:
        copy.start()

    pl.semaphore_wait(barrier, greetings)

    far_copies = [
        pltpu.make_async_remote_copy(
            src_ref=x_hbm.at[m, v],
            dst_ref=far.at[m, v],
            send_sem=far_send.at[m, v],
            recv_sem=far_recv.at[m, v],
            device_id=partner,
            device_id_type=MESH,
        )
        for v in range(count_v)
        for m in range(here)
    ]
    moved = far_copies.pop()
    aside_copy = pltpu.make_async_remote_copy(
        src_ref=x_hbm.at[here - 1, count_v - 1],
        dst_ref=hop,
        send_sem=hop_sems.at[0],
        recv_sem=hop_sems.at[1],
        device_id=(inst, beside),
        device_id_type=MESH,
    )
    onward_copy = pltpu.make_async_remote_copy(
        src_ref=hop,
        dst_ref=far.at[here - 1, count_v - 1],
        send_sem=hop_sems.at[2],
        recv_sem=far_recv.at[here - 1, count_v - 1],
        device_id=(1 - inst, beside),
        device_id_type=MESH,
    )
    started = [0, BATCHES[0], sum(BATCHES), len(far_copies)]

    def start_far(batch):
        for copy in far_copies[started[batch] : started[batch + 1]]:
            copy.start()

    start_far(0)
    for step in STEPS:
        pl.when(below[step])(functools.partial(signal, ack.at[STEPS.index(-step)], at(step)))
    pl.when((inst == 1) & ends)(functools.partial(signal, cross, (1 - inst, beside)))

    for copy in local:
        copy.wait()
    slots = slot[...]
    numbers = lax.broadcasted_iota(jnp.int32, slots.shape, 1)
    mine = slots == me

    def looked_up(mask, values):
        return jnp.sum(jnp.where(mask, values, 0))

    my_rows = looked_up(mine, rows[...])
    picks = []
    shifts = []
    for face in range(2):
        neighbour = looked_up(mine, block[face : face + 1, :])
        neighbour_slot = looked_up(numbers == neighbour, slots)
        distance = lax.rem(neighbour_slot - me + (REACH + span), span)
        picks.append(
            jnp.clip(
                2 * distance + looked_up(mine, side[face : face + 1, :]), 0, rims.shape[0] - 1
            )
        )
        shifts.append(looked_up(mine, shift[face : face + 1, :]))

    high = [jnp.clip(my_rows - 1 - layer, 0, row_count - 1) for layer in range(2)]

    def gather_rim(v, carry):
        for n in range(here):
            rims[2 * OWN, v, 2 * n : 2 * n + 2, :] = near[n, v, 0:2, :]
            for layer in range(2):
                rims[2 * OWN + 1, v, 2 * n + layer : 2 * n + layer + 1, :] = near[
                    n, v, pl.ds(high[layer], 1), :
                ]
        return carry

    lax.fori_loop(0, count_v, gather_rim, 0)

    rim_copies = [
        pltpu.make_async_remote_copy(
            src_ref=rims.at[2 * OWN : 2 * OWN + 2],
            dst_ref=rims.at[2 * (OWN - step) : 2 * (OWN - step) + 2],
            send_sem=rim_send.at[OWN - step],
            recv_sem=rim_recv.at[OWN - step],
            device_id=at(step),
            device_id_type=MESH,
        )
        for step in STEPS
    ]
    def answered(step):
        pl.semaphore_wait(ack.at[STEPS.index(step)], 1)
        rim_copies[STEPS.index(step)].start()

    for step, copy in zip(STEPS, rim_copies):
        pl.when(below[step])(copy.start)
    for step in (1, 2):
        pl.when(above[step])(functools.partial(answered, step))
    pl.when(ends)(aside_copy.start)
    start_far(1)

    def own_source(v, carry):
        values = [near[m, v] for m in range(here)]
        for n in range(here):
            out[n, v] = weighted_sum(
                [-spectral_weight(n - m, instances) for m in range(here)], values
            )
        return carry

    lax.fori_loop(0, count_v, own_source, 0)

    middle = jnp.logical_not(ends)
    pl.when(middle & (inst == 0))(functools.partial(pl.semaphore_wait, cross, 1))

    @pl.when(middle)
    def _():
        aside_copy.wait_recv()
        onward_copy.start()
        moved.start()

    start_far(2)
    for step in (-1, -2):
        pl.when(above[step])(functools.partial(answered, step))
    for copy in rim_copies:
        copy.wait_recv()
    for face in range(2):
        picked = rims[picks[face]]
        amount = columns - shifts[face]
        for v in range(count_v):
            ghosts[face, v] = pltpu.roll(picked[v], amount, 1)

    extent = row_count + 8
    position = lax.broadcasted_iota(jnp.int32, (extent, columns), 0)
    first_beyond = position == my_rows
    second_beyond = position == my_rows + 1
    last_row = lax.broadcasted_iota(jnp.int32, (8, columns), 0) == 7

    def spatial(n, carry):
        fields = []
        for v in range(count_v):
            low = [ghosts[0, v, pl.ds(2 * n + layer, 1), :] for layer in range(2)]
            top = [ghosts[1, v, pl.ds(2 * n + layer, 1), :] for layer in range(2)]
            before = jnp.where(last_row, low[0], low[1])
            block_rows = jnp.concatenate([near[n, v], before], axis=0)
            fields.append(
                jnp.where(first_beyond, top[0], jnp.where(second_beyond, top[1], block_rows))
            )
        inverse = 1.0 / fields[0]
        squares = fields[1] * fields[1] + fields[2] * fields[2] + fields[3] * fields[3]
        pressure = GAMMA_MINUS * (fields[4] - 0.5 * squares * inverse)
        for v, flux in enumerate(flux_parts(fields, pressure, inverse, 1)):
            out[n, v] += differences(flux, fields[v], 0)[:row_count]
        fields = [field[:row_count] for field in fields]
        pressure = pressure[:row_count]
        inverse = inverse[:row_count]
        for v, flux in enumerate(flux_parts(fields, pressure, inverse, 2)):
            out[n, v] += differences(flux, fields[v], 1)
        return carry

    lax.fori_loop(0, here, spatial, 0)

    inside = lax.broadcasted_iota(jnp.int32, (row_count, columns), 0) < my_rows
    for v in range(count_v):
        for copy in (far_copies + [moved])[v * here : (v + 1) * here]:
            copy.wait_recv()
        values = [far[m, v] for m in range(here)]
        for n in range(here):
            source = weighted_sum(
                [spectral_weight(n - m - here, instances) for m in range(here)], values
            )
            out[n, v] = jnp.where(inside, out[n, v] - source, 0.0)
    for copy in far_copies + rim_copies:
        copy.wait_send()
    pl.when(ends)(aside_copy.wait_send)

    @pl.when(jnp.logical_not(ends))
    def _():
        onward_copy.wait_send()
        moved.wait_send()


def on_device(state, slot_of, conn_block, conn_side, conn_shift, rows):
    here, count_v, _, row_count, columns = state.shape
    instances = here * lax.axis_size("inst")
    blocks = slot_of.shape[0]
    whole = (here, count_v, row_count, columns)
    result = pl.pallas_call(
        functools.partial(kernel, instances),
        out_shape=jax.ShapeDtypeStruct(whole, jnp.float32),
        in_specs=[pl.BlockSpec(memory_space=pl.ANY)] * 6,
        out_specs=pl.BlockSpec(memory_space=pltpu.VMEM),
        scratch_shapes=[
            pltpu.VMEM(whole, jnp.float32),
            pltpu.VMEM(whole, jnp.float32),
            pltpu.VMEM((2 * (2 * REACH + 1), count_v, 2 * here, columns), jnp.float32),
            pltpu.VMEM((2, count_v, 2 * here, columns), jnp.float32),
            pltpu.VMEM((1, blocks), jnp.int32),
            pltpu.VMEM((2, blocks), jnp.int32),
            pltpu.VMEM((2, blocks), jnp.int32),
            pltpu.VMEM((2, blocks), jnp.int32),
            pltpu.VMEM((1, blocks), jnp.int32),
            pltpu.SemaphoreType.DMA((6,)),
            pltpu.SemaphoreType.DMA((here, count_v)),
            pltpu.SemaphoreType.DMA((here, count_v)),
            pltpu.SemaphoreType.DMA((2 * REACH + 1,)),
            pltpu.SemaphoreType.DMA((2 * REACH + 1,)),
            pltpu.VMEM((row_count, columns), jnp.float32),
            pltpu.SemaphoreType.DMA((3,)),
            pltpu.SemaphoreType.REGULAR((4,)),
            pltpu.SemaphoreType.REGULAR,
        ],
        compiler_params=pltpu.CompilerParams(
            collective_id=0, has_side_effects=True, vmem_limit_bytes=16 * 2**20
        ),
        name="residual",
    )(
        *[
            pltpu.with_memory_space_constraint(operand, pltpu.HBM)
            for operand in (
                state.reshape(whole),
                slot_of.reshape(1, blocks),
                conn_block.T,
                conn_side.T,
                conn_shift.T,
                rows.reshape(1, blocks),
            )
        ]
    )
    return result.reshape(state.shape)


def solution(mesh):
    in_specs = (P("inst", None, "blk", None, None), P(), P(), P(), P(), P())
    out_specs = P("inst", None, "blk", None, None)
    return jax.shard_map(
        on_device, mesh=mesh, in_specs=in_specs, out_specs=out_specs, check_vma=False
    )
```

```python
import functools
import math

import jax
import jax.numpy as jnp
from jax import lax
from jax.experimental import pallas as pl
from jax.experimental.pallas import tpu as pltpu
from jax.sharding import PartitionSpec as P

REACH = 2
GAMMA_MINUS = 0.4
DAMPING = 0.05
FREQUENCY = 1.0
MESH = pl.DeviceIdType.MESH
OWN = REACH
STEPS = (-2, 2, -1, 1)
EARLY = 6
HELD = 3
ASIDE = 2


def spectral_weight(offset, count):
    offset %= count
    if offset == 0 or 2 * offset == count:
        return 0.0
    return 0.5 * FREQUENCY * (-1.0) ** offset / math.tan(math.pi * offset / count)


def weighted_sum(weights, values):
    total = None
    for weight, value in zip(weights, values):
        if weight == 0.0:
            continue
        term = weight * value
        total = term if total is None else total + term
    return total


def differences(flux, fields, axis):
    size = fields.shape[axis]
    wide = flux * (8.0 / 12.0)
    narrow = flux * (1.0 / 12.0)
    near = fields * (4.0 * DAMPING)
    far = fields * DAMPING
    ahead = (near - wide) + pltpu.roll(narrow - far, size - 1, axis)
    behind = (near + wide) - pltpu.roll(narrow + far, 1, axis)
    return (
        pltpu.roll(ahead, size - 1, axis)
        + pltpu.roll(behind, 1, axis)
        - fields * (6.0 * DAMPING)
    )


def flux_parts(fields, pressure, inverse, direction):
    velocity = fields[direction] * inverse
    parts = [
        fields[direction],
        fields[1] * velocity,
        fields[2] * velocity,
        fields[3] * velocity,
        (fields[4] + pressure) * velocity,
    ]
    parts[direction] = parts[direction] + pressure
    return parts


def kernel(
    instances, x_hbm, slot_hbm, block_hbm, side_hbm, shift_hbm, rows_hbm, out,
    near, far, rims, ghosts, slot, block, side, shift, rows,
    in_sems, far_send, far_recv, rim_send, rim_recv, hop, hop_sems, ack, cross,
):
    here, count_v, row_count, columns = near.shape
    inst = lax.axis_index("inst")
    me = lax.axis_index("blk")
    span = lax.axis_size("blk")
    partner = (1 - inst, me)
    place = lax.rem(me // 2, 4)

    def at(step):
        return (inst, lax.rem(me + step + span, span))

    ends = (place == 0) | (place == 3)
    aside = 2 - 4 * lax.rem(place, 2)
    beside = lax.rem(me + aside + span, span)

    def signal(semaphore, device):
        pl.semaphore_signal(semaphore, inc=1, device_id=device, device_id_type=MESH)

    below = {step: lax.rem(me + step + span, span) < me for step in STEPS}
    above = {step: lax.rem(me + step + span, span) > me for step in STEPS}
    barrier = pltpu.get_barrier_semaphore()
    signal(barrier, partner)
    for step in STEPS:
        pl.when(above[step])(functools.partial(signal, barrier, at(step)))
    pl.when(inst == 0)(functools.partial(signal, barrier, (1 - inst, beside)))
    greetings = 1 + inst
    for step in STEPS:
        greetings = greetings + jnp.where(below[step], 1, 0)

    local = [
        pltpu.make_async_copy(source, target, in_sems.at[index])
        for index, (source, target) in enumerate(
            [
                (slot_hbm, slot),
                (rows_hbm, rows),
                (block_hbm, block),
                (side_hbm, side),
                (shift_hbm, shift),
                (x_hbm, near),
            ]
        )
    ]
    for copy in local:
        copy.start()

    pl.semaphore_wait(barrier, greetings)

    far_copies = [
        pltpu.make_async_remote_copy(
            src_ref=x_hbm.at[m, v],
            dst_ref=far.at[m, v],
            send_sem=far_send.at[m, v],
            recv_sem=far_recv.at[m, v],
            device_id=partner,
            device_id_type=MESH,
        )
        for v in range(count_v)
        for m in range(here)
    ]
    middle = jnp.logical_not(ends)
    sends = [ends, place == 0]
    passes = [middle, place == 1]
    always = far_copies[: len(far_copies) - ASIDE]
    moved = far_copies[: len(always) - 1 : -1]
    aside_copies = []
    onward_copies = []
    for piece in range(ASIDE):
        v, m = divmod(len(far_copies) - 1 - piece, here)
        aside_copies.append(
            pltpu.make_async_remote_copy(
                src_ref=x_hbm.at[m, v],
                dst_ref=hop.at[piece],
                send_sem=hop_sems.at[0, piece],
                recv_sem=hop_sems.at[1, piece],
                device_id=(inst, beside),
                device_id_type=MESH,
            )
        )
        onward_copies.append(
            pltpu.make_async_remote_copy(
                src_ref=hop.at[piece],
                dst_ref=far.at[m, v],
                send_sem=hop_sems.at[2, piece],
                recv_sem=far_recv.at[m, v],
                device_id=(1 - inst, beside),
                device_id_type=MESH,
            )
        )
    for copy in always[:EARLY]:
        copy.start()
    for step in STEPS:
        pl.when(below[step])(functools.partial(signal, ack.at[STEPS.index(-step)], at(step)))
    pl.when((inst == 1) & ends)(functools.partial(signal, cross, (1 - inst, beside)))

    for copy in local:
        copy.wait()
    slots = slot[...]
    numbers = lax.broadcasted_iota(jnp.int32, slots.shape, 1)
    mine = slots == me

    def looked_up(mask, values):
        return jnp.sum(jnp.where(mask, values, 0))

    my_rows = looked_up(mine, rows[...])
    picks = []
    shifts = []
    for face in range(2):
        neighbour = looked_up(mine, block[face : face + 1, :])
        neighbour_slot = looked_up(numbers == neighbour, slots)
        distance = lax.rem(neighbour_slot - me + (REACH + span), span)
        picks.append(
            jnp.clip(
                2 * distance + looked_up(mine, side[face : face + 1, :]), 0, rims.shape[0] - 1
            )
        )
        shifts.append(looked_up(mine, shift[face : face + 1, :]))

    high = [jnp.clip(my_rows - 1 - layer, 0, row_count - 1) for layer in range(2)]

    def gather_rim(v, carry):
        for n in range(here):
            rims[2 * OWN, v, 2 * n : 2 * n + 2, :] = near[n, v, 0:2, :]
            for layer in range(2):
                rims[2 * OWN + 1, v, 2 * n + layer : 2 * n + layer + 1, :] = near[
                    n, v, pl.ds(high[layer], 1), :
                ]
        return carry

    lax.fori_loop(0, count_v, gather_rim, 0)

    rim_copies = [
        pltpu.make_async_remote_copy(
            src_ref=rims.at[2 * OWN : 2 * OWN + 2],
            dst_ref=rims.at[2 * (OWN - step) : 2 * (OWN - step) + 2],
            send_sem=rim_send.at[OWN - step],
            recv_sem=rim_recv.at[OWN - step],
            device_id=at(step),
            device_id_type=MESH,
        )
        for step in STEPS
    ]
    def answered(step):
        pl.semaphore_wait(ack.at[STEPS.index(step)], 1)
        rim_copies[STEPS.index(step)].start()

    for step, copy in zip(STEPS, rim_copies):
        pl.when(below[step])(copy.start)
    for step in (1, 2):
        pl.when(above[step])(functools.partial(answered, step))
    for piece in range(ASIDE):
        pl.when(sends[piece])(aside_copies[piece].start)
    for copy in always[EARLY : len(always) - HELD]:
        copy.start()

    def own_source(v, carry):
        values = [near[m, v] for m in range(here)]
        for n in range(here):
            out[n, v] = weighted_sum(
                [-spectral_weight(n - m, instances) for m in range(here)], values
            )
        return carry

    lax.fori_loop(0, count_v, own_source, 0)

    pl.when(middle & (inst == 0))(functools.partial(pl.semaphore_wait, cross, 1))

    def pass_on(piece):
        aside_copies[piece].wait_recv()
        onward_copies[piece].start()

    for piece in range(ASIDE):
        pl.when(passes[piece])(functools.partial(pass_on, piece))
    for copy in always[len(always) - HELD :]:
        copy.start()
    for piece in range(ASIDE):
        pl.when(jnp.logical_not(sends[piece]))(moved[piece].start)
    for step in (-1, -2):
        pl.when(above[step])(functools.partial(answered, step))
    for copy in rim_copies:
        copy.wait_recv()
    for face in range(2):
        picked = rims[picks[face]]
        amount = columns - shifts[face]
        for v in range(count_v):
            ghosts[face, v] = pltpu.roll(picked[v], amount, 1)

    extent = row_count + 8
    position = lax.broadcasted_iota(jnp.int32, (extent, columns), 0)
    first_beyond = position == my_rows
    second_beyond = position == my_rows + 1
    last_row = lax.broadcasted_iota(jnp.int32, (8, columns), 0) == 7

    def spatial(n, carry):
        fields = []
        for v in range(count_v):
            low = [ghosts[0, v, pl.ds(2 * n + layer, 1), :] for layer in range(2)]
            top = [ghosts[1, v, pl.ds(2 * n + layer, 1), :] for layer in range(2)]
            before = jnp.where(last_row, low[0], low[1])
            block_rows = jnp.concatenate([near[n, v], before], axis=0)
            fields.append(
                jnp.where(first_beyond, top[0], jnp.where(second_beyond, top[1], block_rows))
            )
        inverse = 1.0 / fields[0]
        squares = fields[1] * fields[1] + fields[2] * fields[2] + fields[3] * fields[3]
        pressure = GAMMA_MINUS * (fields[4] - 0.5 * squares * inverse)
        for v, flux in enumerate(flux_parts(fields, pressure, inverse, 1)):
            out[n, v] += differences(flux, fields[v], 0)[:row_count]
        fields = [field[:row_count] for field in fields]
        pressure = pressure[:row_count]
        inverse = inverse[:row_count]
        for v, flux in enumerate(flux_parts(fields, pressure, inverse, 2)):
            out[n, v] += differences(flux, fields[v], 1)
        return carry

    lax.fori_loop(0, here, spatial, 0)

    inside = lax.broadcasted_iota(jnp.int32, (row_count, columns), 0) < my_rows
    for v in range(count_v):
        for copy in far_copies[v * here : (v + 1) * here]:
            copy.wait_recv()
        values = [far[m, v] for m in range(here)]
        for n in range(here):
            source = weighted_sum(
                [spectral_weight(n - m - here, instances) for m in range(here)], values
            )
            out[n, v] = jnp.where(inside, out[n, v] - source, 0.0)
    for copy in always + rim_copies:
        copy.wait_send()
    for piece in range(ASIDE):
        pl.when(sends[piece])(aside_copies[piece].wait_send)
        pl.when(passes[piece])(onward_copies[piece].wait_send)
        pl.when(jnp.logical_not(sends[piece]))(moved[piece].wait_send)


def on_device(state, slot_of, conn_block, conn_side, conn_shift, rows):
    here, count_v, _, row_count, columns = state.shape
    instances = here * lax.axis_size("inst")
    blocks = slot_of.shape[0]
    whole = (here, count_v, row_count, columns)
    result = pl.pallas_call(
        functools.partial(kernel, instances),
        out_shape=jax.ShapeDtypeStruct(whole, jnp.float32),
        in_specs=[pl.BlockSpec(memory_space=pl.ANY)] * 6,
        out_specs=pl.BlockSpec(memory_space=pltpu.VMEM),
        scratch_shapes=[
            pltpu.VMEM(whole, jnp.float32),
            pltpu.VMEM(whole, jnp.float32),
            pltpu.VMEM((2 * (2 * REACH + 1), count_v, 2 * here, columns), jnp.float32),
            pltpu.VMEM((2, count_v, 2 * here, columns), jnp.float32),
            pltpu.VMEM((1, blocks), jnp.int32),
            pltpu.VMEM((2, blocks), jnp.int32),
            pltpu.VMEM((2, blocks), jnp.int32),
            pltpu.VMEM((2, blocks), jnp.int32),
            pltpu.VMEM((1, blocks), jnp.int32),
            pltpu.SemaphoreType.DMA((6,)),
            pltpu.SemaphoreType.DMA((here, count_v)),
            pltpu.SemaphoreType.DMA((here, count_v)),
            pltpu.SemaphoreType.DMA((2 * REACH + 1,)),
            pltpu.SemaphoreType.DMA((2 * REACH + 1,)),
            pltpu.VMEM((ASIDE, row_count, columns), jnp.float32),
            pltpu.SemaphoreType.DMA((3, ASIDE)),
            pltpu.SemaphoreType.REGULAR((4,)),
            pltpu.SemaphoreType.REGULAR,
        ],
        compiler_params=pltpu.CompilerParams(
            collective_id=0, has_side_effects=True, vmem_limit_bytes=16 * 2**20
        ),
        name="residual",
    )(
        *[
            pltpu.with_memory_space_constraint(operand, pltpu.HBM)
            for operand in (
                state.reshape(whole),
                slot_of.reshape(1, blocks),
                conn_block.T,
                conn_side.T,
                conn_shift.T,
                rows.reshape(1, blocks),
            )
        ]
    )
    return result.reshape(state.shape)


def solution(mesh):
    in_specs = (P("inst", None, "blk", None, None), P(), P(), P(), P(), P())
    out_specs = P("inst", None, "blk", None, None)
    return jax.shard_map(
        on_device, mesh=mesh, in_specs=in_specs, out_specs=out_specs, check_vma=False
    )
```

```python
import functools
import math

import jax
import jax.numpy as jnp
from jax import lax
from jax.experimental import pallas as pl
from jax.experimental.pallas import tpu as pltpu
from jax.sharding import PartitionSpec as P

REACH = 2
GAMMA_MINUS = 0.4
DAMPING = 0.05
FREQUENCY = 1.0
MESH = pl.DeviceIdType.MESH
OWN = REACH
STEPS = (-2, 2, -1, 1)
EARLY = 6
HELD = 3
ASIDE = 2
FIRST_ROW = 8


def spectral_weight(offset, count):
    offset %= count
    if offset == 0 or 2 * offset == count:
        return 0.0
    return 0.5 * FREQUENCY * (-1.0) ** offset / math.tan(math.pi * offset / count)


def weighted_sum(weights, values):
    total = None
    for weight, value in zip(weights, values):
        if weight == 0.0:
            continue
        term = weight * value
        total = term if total is None else total + term
    return total


def differences(flux, fields, axis):
    size = fields.shape[axis]
    wide = flux * (8.0 / 12.0)
    narrow = flux * (1.0 / 12.0)
    near = fields * (4.0 * DAMPING)
    far = fields * DAMPING
    ahead = (near - wide) + pltpu.roll(narrow - far, size - 1, axis)
    behind = (near + wide) - pltpu.roll(narrow + far, 1, axis)
    return (
        pltpu.roll(ahead, size - 1, axis)
        + pltpu.roll(behind, 1, axis)
        - fields * (6.0 * DAMPING)
    )


def flux_parts(fields, pressure, inverse, direction):
    velocity = fields[direction] * inverse
    parts = [
        fields[direction],
        fields[1] * velocity,
        fields[2] * velocity,
        fields[3] * velocity,
        (fields[4] + pressure) * velocity,
    ]
    parts[direction] = parts[direction] + pressure
    return parts


def kernel(
    instances, x_hbm, slot_hbm, block_hbm, side_hbm, shift_hbm, rows_hbm, out,
    near, far, rims, ghosts, slot, block, side, shift, rows,
    in_sems, far_send, far_recv, rim_send, rim_recv, hop, hop_sems, ack, cross, helper, share_sem,
):
    here, count_v, row_count, columns = near.shape
    inst = lax.axis_index("inst")
    me = lax.axis_index("blk")
    span = lax.axis_size("blk")
    partner = (1 - inst, me)
    place = lax.rem(me // 2, 4)

    def at(step):
        return (inst, lax.rem(me + step + span, span))

    rest = me >= FIRST_ROW
    first = rest & (place == 0)
    helps = [rest & (place == piece + 1) for piece in range(ASIDE)]
    beside = [
        lax.rem(me + (2 + 2 * piece) * jnp.where(place == 0, 1, -1) + span, span)
        for piece in range(ASIDE)
    ]

    def signal(semaphore, device):
        pl.semaphore_signal(semaphore, inc=1, device_id=device, device_id_type=MESH)

    def order(index):
        return jnp.where(index == 0, 5, 2 * index)

    below = {step: order(lax.rem(me + step + span, span)) < order(me) for step in STEPS}
    above = {step: jnp.logical_not(below[step]) for step in STEPS}
    barrier = pltpu.get_barrier_semaphore()
    signal(barrier, partner)
    for step in STEPS:
        pl.when(above[step])(functools.partial(signal, barrier, at(step)))
    greetings = 1 + jnp.where(helps[1], 1, 0)
    pl.when(first)(functools.partial(signal, barrier, (inst, beside[1])))
    for piece in range(ASIDE):
        takes_part = first | helps[piece]
        greetings = greetings + inst * jnp.where(takes_part, 1, 0)
        pl.when((inst == 0) & takes_part)(
            functools.partial(signal, barrier, (1 - inst, beside[piece]))
        )
    for step in STEPS:
        greetings = greetings + jnp.where(below[step], 1, 0)

    local = [
        pltpu.make_async_copy(source, target, in_sems.at[index])
        for index, (source, target) in enumerate(
            [
                (slot_hbm, slot),
                (rows_hbm, rows),
                (block_hbm, block),
                (side_hbm, side),
                (shift_hbm, shift),
                (x_hbm, near),
            ]
        )
    ]
    for copy in local:
        copy.start()

    pl.semaphore_wait(barrier, greetings)

    far_copies = [
        pltpu.make_async_remote_copy(
            src_ref=x_hbm.at[m, v],
            dst_ref=far.at[m, v],
            send_sem=far_send.at[m, v],
            recv_sem=far_recv.at[m, v],
            device_id=partner,
            device_id_type=MESH,
        )
        for v in range(count_v)
        for m in range(here)
    ]
    always = far_copies[: len(far_copies) - ASIDE]
    moved = far_copies[: len(always) - 1 : -1]
    aside_copies = []
    onward_copies = []
    for piece in range(ASIDE):
        v, m = divmod(len(far_copies) - 1 - piece, here)
        aside_copies.append(
            pltpu.make_async_remote_copy(
                src_ref=x_hbm.at[m, v],
                dst_ref=hop.at[piece],
                send_sem=hop_sems.at[0, piece],
                recv_sem=hop_sems.at[1, piece],
                device_id=(inst, beside[piece]),
                device_id_type=MESH,
            )
        )
        onward_copies.append(
            pltpu.make_async_remote_copy(
                src_ref=hop.at[piece],
                dst_ref=far.at[m, v],
                send_sem=hop_sems.at[2, piece],
                recv_sem=far_recv.at[m, v],
                device_id=(1 - inst, beside[piece]),
                device_id_type=MESH,
            )
        )
    for copy in always[:EARLY]:
        copy.start()
    for step in STEPS:
        pl.when(below[step])(functools.partial(signal, ack.at[STEPS.index(-step)], at(step)))
    pl.when(helps[1])(functools.partial(signal, helper, (inst, beside[1])))
    for piece in range(ASIDE):
        pl.when((inst == 1) & first)(functools.partial(signal, cross, (1 - inst, beside[piece])))

    for copy in local:
        copy.wait()
    slots = slot[...]
    numbers = lax.broadcasted_iota(jnp.int32, slots.shape, 1)
    mine = slots == me

    def looked_up(mask, values):
        return jnp.sum(jnp.where(mask, values, 0))

    my_rows = looked_up(mine, rows[...])
    picks = []
    shifts = []
    for face in range(2):
        neighbour = looked_up(mine, block[face : face + 1, :])
        neighbour_slot = looked_up(numbers == neighbour, slots)
        distance = lax.rem(neighbour_slot - me + (REACH + span), span)
        picks.append(
            jnp.clip(
                2 * distance + looked_up(mine, side[face : face + 1, :]), 0, rims.shape[0] - 1
            )
        )
        shifts.append(looked_up(mine, shift[face : face + 1, :]))

    high = [jnp.clip(my_rows - 1 - layer, 0, row_count - 1) for layer in range(2)]

    def gather_rim(v, carry):
        for n in range(here):
            rims[2 * OWN, v, 2 * n : 2 * n + 2, :] = near[n, v, 0:2, :]
            for layer in range(2):
                rims[2 * OWN + 1, v, 2 * n + layer : 2 * n + layer + 1, :] = near[
                    n, v, pl.ds(high[layer], 1), :
                ]
        return carry

    lax.fori_loop(0, count_v, gather_rim, 0)

    rim_copies = [
        pltpu.make_async_remote_copy(
            src_ref=rims.at[2 * OWN : 2 * OWN + 2],
            dst_ref=rims.at[2 * (OWN - step) : 2 * (OWN - step) + 2],
            send_sem=rim_send.at[OWN - step],
            recv_sem=rim_recv.at[OWN - step],
            device_id=at(step),
            device_id_type=MESH,
        )
        for step in STEPS
    ]
    core = lax.rem(me, 2)
    whole = {step: place >= 0 for step in STEPS}
    whole[1] = jnp.logical_not((place == 3) & (core == 1))
    whole[-1] = jnp.logical_not((place == 0) & (core == 0))
    shares = ((place == 0) & (core == 1)) | ((place == 3) & (core == 0))
    shared_copy = pltpu.make_async_remote_copy(
        src_ref=rims.at[pl.ds(8 * (1 - core), 2)],
        dst_ref=rims.at[pl.ds(6 - 4 * core, 2)],
        send_sem=share_sem,
        recv_sem=rim_recv.at[3 - 2 * core],
        device_id=(inst, me + 1 - 2 * core),
        device_id_type=MESH,
    )

    def answered(step):
        pl.semaphore_wait(ack.at[STEPS.index(step)], 1)
        pl.when(whole[step])(rim_copies[STEPS.index(step)].start)

    for step, copy in zip(STEPS, rim_copies):
        pl.when(below[step] & whole[step])(copy.start)
    for step in (1, 2):
        pl.when(above[step])(functools.partial(answered, step))

    @pl.when(first)
    def _():
        pl.semaphore_wait(helper, 1)
        for copy in aside_copies:
            copy.start()

    for copy in always[EARLY : len(always) - HELD]:
        copy.start()

    def own_source(v, carry):
        values = [near[m, v] for m in range(here)]
        for n in range(here):
            out[n, v] = weighted_sum(
                [-spectral_weight(n - m, instances) for m in range(here)], values
            )
        return carry

    lax.fori_loop(0, count_v, own_source, 0)

    pl.when((helps[0] | helps[1]) & (inst == 0))(functools.partial(pl.semaphore_wait, cross, 1))

    def pass_on(piece):
        aside_copies[piece].wait_recv()
        onward_copies[piece].start()

    for piece in range(ASIDE):
        pl.when(helps[piece])(functools.partial(pass_on, piece))
    for copy in always[len(always) - HELD :]:
        copy.start()
    for copy in moved:
        pl.when(jnp.logical_not(first))(copy.start)
    for step in (-1, -2):
        pl.when(above[step])(functools.partial(answered, step))
    two_back = rim_copies[STEPS.index(2)]
    two_ahead = rim_copies[STEPS.index(-2)]
    two_back.wait_recv()
    two_ahead.wait_recv()
    pl.when(shares)(shared_copy.start)
    for step in (1, -1):
        rim_copies[STEPS.index(step)].wait_recv()
    for face in range(2):
        picked = rims[picks[face]]
        amount = columns - shifts[face]
        for v in range(count_v):
            ghosts[face, v] = pltpu.roll(picked[v], amount, 1)

    extent = row_count + 8
    position = lax.broadcasted_iota(jnp.int32, (extent, columns), 0)
    first_beyond = position == my_rows
    second_beyond = position == my_rows + 1
    last_row = lax.broadcasted_iota(jnp.int32, (8, columns), 0) == 7

    def spatial(n, carry):
        fields = []
        for v in range(count_v):
            low = [ghosts[0, v, pl.ds(2 * n + layer, 1), :] for layer in range(2)]
            top = [ghosts[1, v, pl.ds(2 * n + layer, 1), :] for layer in range(2)]
            before = jnp.where(last_row, low[0], low[1])
            block_rows = jnp.concatenate([near[n, v], before], axis=0)
            fields.append(
                jnp.where(first_beyond, top[0], jnp.where(second_beyond, top[1], block_rows))
            )
        inverse = 1.0 / fields[0]
        squares = fields[1] * fields[1] + fields[2] * fields[2] + fields[3] * fields[3]
        pressure = GAMMA_MINUS * (fields[4] - 0.5 * squares * inverse)
        for v, flux in enumerate(flux_parts(fields, pressure, inverse, 1)):
            out[n, v] += differences(flux, fields[v], 0)[:row_count]
        fields = [field[:row_count] for field in fields]
        pressure = pressure[:row_count]
        inverse = inverse[:row_count]
        for v, flux in enumerate(flux_parts(fields, pressure, inverse, 2)):
            out[n, v] += differences(flux, fields[v], 1)
        return carry

    lax.fori_loop(0, here, spatial, 0)

    inside = lax.broadcasted_iota(jnp.int32, (row_count, columns), 0) < my_rows
    for v in range(count_v):
        for copy in far_copies[v * here : (v + 1) * here]:
            copy.wait_recv()
        values = [far[m, v] for m in range(here)]
        for n in range(here):
            source = weighted_sum(
                [spectral_weight(n - m - here, instances) for m in range(here)], values
            )
            out[n, v] = jnp.where(inside, out[n, v] - source, 0.0)
    for copy in always:
        copy.wait_send()
    for step, copy in zip(STEPS, rim_copies):
        pl.when(whole[step])(copy.wait_send)
    pl.when(shares)(shared_copy.wait_send)
    for piece in range(ASIDE):
        pl.when(first)(aside_copies[piece].wait_send)
        pl.when(helps[piece])(onward_copies[piece].wait_send)
        pl.when(jnp.logical_not(first))(moved[piece].wait_send)


def on_device(state, slot_of, conn_block, conn_side, conn_shift, rows):
    here, count_v, _, row_count, columns = state.shape
    instances = here * lax.axis_size("inst")
    blocks = slot_of.shape[0]
    whole = (here, count_v, row_count, columns)
    result = pl.pallas_call(
        functools.partial(kernel, instances),
        out_shape=jax.ShapeDtypeStruct(whole, jnp.float32),
        in_specs=[pl.BlockSpec(memory_space=pl.ANY)] * 6,
        out_specs=pl.BlockSpec(memory_space=pltpu.VMEM),
        scratch_shapes=[
            pltpu.VMEM(whole, jnp.float32),
            pltpu.VMEM(whole, jnp.float32),
            pltpu.VMEM((2 * (2 * REACH + 1), count_v, 2 * here, columns), jnp.float32),
            pltpu.VMEM((2, count_v, 2 * here, columns), jnp.float32),
            pltpu.VMEM((1, blocks), jnp.int32),
            pltpu.VMEM((2, blocks), jnp.int32),
            pltpu.VMEM((2, blocks), jnp.int32),
            pltpu.VMEM((2, blocks), jnp.int32),
            pltpu.VMEM((1, blocks), jnp.int32),
            pltpu.SemaphoreType.DMA((6,)),
            pltpu.SemaphoreType.DMA((here, count_v)),
            pltpu.SemaphoreType.DMA((here, count_v)),
            pltpu.SemaphoreType.DMA((2 * REACH + 1,)),
            pltpu.SemaphoreType.DMA((2 * REACH + 1,)),
            pltpu.VMEM((ASIDE, row_count, columns), jnp.float32),
            pltpu.SemaphoreType.DMA((3, ASIDE)),
            pltpu.SemaphoreType.REGULAR((4,)),
            pltpu.SemaphoreType.REGULAR,
            pltpu.SemaphoreType.REGULAR,
            pltpu.SemaphoreType.DMA,
        ],
        compiler_params=pltpu.CompilerParams(
            collective_id=0, has_side_effects=True, vmem_limit_bytes=16 * 2**20
        ),
        name="residual",
    )(
        *[
            pltpu.with_memory_space_constraint(operand, pltpu.HBM)
            for operand in (
                state.reshape(whole),
                slot_of.reshape(1, blocks),
                conn_block.T,
                conn_side.T,
                conn_shift.T,
                rows.reshape(1, blocks),
            )
        ]
    )
    return result.reshape(state.shape)


def solution(mesh):
    in_specs = (P("inst", None, "blk", None, None), P(), P(), P(), P(), P())
    out_specs = P("inst", None, "blk", None, None)
    return jax.shard_map(
        on_device, mesh=mesh, in_specs=in_specs, out_specs=out_specs, check_vma=False
    )
```

```python
import functools
import math

import jax
import jax.numpy as jnp
from jax import lax
from jax.experimental import pallas as pl
from jax.experimental.pallas import tpu as pltpu
from jax.sharding import PartitionSpec as P

REACH = 2
GAMMA_MINUS = 0.4
DAMPING = 0.05
FREQUENCY = 1.0
MESH = pl.DeviceIdType.MESH
OWN = REACH
STEPS = (-2, 2, -1, 1)
EARLY = 6
HELD = 3
ASIDE = 2
FIRST_ROW = 8


def spectral_weight(offset, count):
    offset %= count
    if offset == 0:
        return 0.0
    return 0.5 * FREQUENCY * (-1.0) ** offset / math.tan(math.pi * offset / count)


def weighted_sum(weights, values):
    total = None
    for weight, value in zip(weights, values):
        if weight == 0.0:
            continue
        term = weight * value
        total = term if total is None else total + term
    return total


def differences(flux, fields, axis):
    size = fields.shape[axis]
    wide = flux * (8.0 / 12.0)
    narrow = flux * (1.0 / 12.0)
    near = fields * (4.0 * DAMPING)
    far = fields * DAMPING
    ahead = (near - wide) + pltpu.roll(narrow - far, size - 1, axis)
    behind = (near + wide) - pltpu.roll(narrow + far, 1, axis)
    return (
        pltpu.roll(ahead, size - 1, axis)
        + pltpu.roll(behind, 1, axis)
        - fields * (6.0 * DAMPING)
    )


def flux_parts(fields, pressure, inverse, direction):
    velocity = fields[direction] * inverse
    parts = [
        fields[direction],
        fields[1] * velocity,
        fields[2] * velocity,
        fields[3] * velocity,
        (fields[4] + pressure) * velocity,
    ]
    parts[direction] = parts[direction] + pressure
    return parts


def kernel(
    instances, x_hbm, slot_hbm, block_hbm, side_hbm, shift_hbm, rows_hbm, out,
    near, far, rims, ghosts, slot, block, side, shift, rows,
    in_sems, far_send, far_recv, rim_send, rim_recv, hop, hop_sems, ack, cross, helper, share_sem,
):
    here, count_v, row_count, columns = near.shape
    inst = lax.axis_index("inst")
    me = lax.axis_index("blk")
    span = lax.axis_size("blk")
    partner = (1 - inst, me)
    place = lax.rem(me // 2, 4)

    def at(step):
        return (inst, lax.rem(me + step + span, span))

    rest = me >= FIRST_ROW
    first = rest & (place == 0)
    helps = [rest & (place == piece + 1) for piece in range(ASIDE)]
    beside = [
        lax.rem(me + (2 + 2 * piece) * jnp.where(place == 0, 1, -1) + span, span)
        for piece in range(ASIDE)
    ]

    def signal(semaphore, device):
        pl.semaphore_signal(semaphore, inc=1, device_id=device, device_id_type=MESH)

    def order(index):
        return jnp.where(index == 0, 5, 2 * index)

    below = {step: order(lax.rem(me + step + span, span)) < order(me) for step in STEPS}
    above = {step: jnp.logical_not(below[step]) for step in STEPS}
    barrier = pltpu.get_barrier_semaphore()
    signal(barrier, partner)
    for step in STEPS:
        pl.when(above[step])(functools.partial(signal, barrier, at(step)))
    greetings = 1 + jnp.where(helps[1], 1, 0)
    pl.when(first)(functools.partial(signal, barrier, (inst, beside[1])))
    for piece in range(ASIDE):
        takes_part = first | helps[piece]
        greetings = greetings + inst * jnp.where(takes_part, 1, 0)
        pl.when((inst == 0) & takes_part)(
            functools.partial(signal, barrier, (1 - inst, beside[piece]))
        )
    for step in STEPS:
        greetings = greetings + jnp.where(below[step], 1, 0)

    local = [
        pltpu.make_async_copy(source, target, in_sems.at[index])
        for index, (source, target) in enumerate(
            [
                (slot_hbm, slot),
                (rows_hbm, rows),
                (block_hbm, block),
                (side_hbm, side),
                (shift_hbm, shift),
                (x_hbm, near),
            ]
        )
    ]
    pl.semaphore_wait(barrier, greetings)

    far_copies = [
        pltpu.make_async_remote_copy(
            src_ref=x_hbm.at[m, v],
            dst_ref=far.at[m, v],
            send_sem=far_send.at[m, v],
            recv_sem=far_recv.at[m, v],
            device_id=partner,
            device_id_type=MESH,
        )
        for v in range(count_v)
        for m in range(here)
    ]
    always = far_copies[: len(far_copies) - ASIDE]
    moved = far_copies[: len(always) - 1 : -1]
    aside_copies = []
    onward_copies = []
    for piece in range(ASIDE):
        v, m = divmod(len(far_copies) - 1 - piece, here)
        aside_copies.append(
            pltpu.make_async_remote_copy(
                src_ref=x_hbm.at[m, v],
                dst_ref=hop.at[piece],
                send_sem=hop_sems.at[0, piece],
                recv_sem=hop_sems.at[1, piece],
                device_id=(inst, beside[piece]),
                device_id_type=MESH,
            )
        )
        onward_copies.append(
            pltpu.make_async_remote_copy(
                src_ref=hop.at[piece],
                dst_ref=far.at[m, v],
                send_sem=hop_sems.at[2, piece],
                recv_sem=far_recv.at[m, v],
                device_id=(1 - inst, beside[piece]),
                device_id_type=MESH,
            )
        )
    for copy in always[:EARLY]:
        copy.start()
    for copy in local:
        copy.start()
    for step in STEPS:
        pl.when(below[step])(functools.partial(signal, ack.at[STEPS.index(-step)], at(step)))
    pl.when(helps[1])(functools.partial(signal, helper, (inst, beside[1])))
    for piece in range(ASIDE):
        pl.when((inst == 1) & first)(functools.partial(signal, cross, (1 - inst, beside[piece])))

    for copy in local:
        copy.wait()
    slots = slot[...]
    numbers = lax.broadcasted_iota(jnp.int32, slots.shape, 1)
    mine = slots == me

    def looked_up(mask, values):
        return jnp.sum(jnp.where(mask, values, 0))

    my_rows = looked_up(mine, rows[...])
    picks = []
    shifts = []
    for face in range(2):
        neighbour = looked_up(mine, block[face : face + 1, :])
        neighbour_slot = looked_up(numbers == neighbour, slots)
        distance = lax.rem(neighbour_slot - me + (REACH + span), span)
        picks.append(
            jnp.clip(
                2 * distance + looked_up(mine, side[face : face + 1, :]), 0, rims.shape[0] - 1
            )
        )
        shifts.append(looked_up(mine, shift[face : face + 1, :]))

    high = [jnp.clip(my_rows - 1 - layer, 0, row_count - 1) for layer in range(2)]

    def gather_rim(v, carry):
        for n in range(here):
            rims[2 * OWN, v, 2 * n : 2 * n + 2, :] = near[n, v, 0:2, :]
            for layer in range(2):
                rims[2 * OWN + 1, v, 2 * n + layer : 2 * n + layer + 1, :] = near[
                    n, v, pl.ds(high[layer], 1), :
                ]
        return carry

    lax.fori_loop(0, count_v, gather_rim, 0)

    rim_copies = [
        pltpu.make_async_remote_copy(
            src_ref=rims.at[2 * OWN : 2 * OWN + 2],
            dst_ref=rims.at[2 * (OWN - step) : 2 * (OWN - step) + 2],
            send_sem=rim_send.at[OWN - step],
            recv_sem=rim_recv.at[OWN - step],
            device_id=at(step),
            device_id_type=MESH,
        )
        for step in STEPS
    ]
    core = lax.rem(me, 2)
    whole = {step: place >= 0 for step in STEPS}
    whole[1] = jnp.logical_not((place == 3) & (core == 1))
    whole[-1] = jnp.logical_not((place == 0) & (core == 0))
    shares = ((place == 0) & (core == 1)) | ((place == 3) & (core == 0))
    shared_copy = pltpu.make_async_remote_copy(
        src_ref=rims.at[pl.ds(8 * (1 - core), 2)],
        dst_ref=rims.at[pl.ds(6 - 4 * core, 2)],
        send_sem=share_sem,
        recv_sem=rim_recv.at[3 - 2 * core],
        device_id=(inst, me + 1 - 2 * core),
        device_id_type=MESH,
    )

    def answered(step):
        pl.semaphore_wait(ack.at[STEPS.index(step)], 1)
        pl.when(whole[step])(rim_copies[STEPS.index(step)].start)

    for step, copy in zip(STEPS, rim_copies):
        pl.when(below[step] & whole[step])(copy.start)
    for step in (1, 2):
        pl.when(above[step])(functools.partial(answered, step))

    @pl.when(first)
    def _():
        pl.semaphore_wait(helper, 1)
        for copy in aside_copies:
            copy.start()

    for copy in always[EARLY : len(always) - HELD]:
        copy.start()

    def own_source(v, carry):
        values = [near[m, v] for m in range(here)]
        for n in range(here):
            out[n, v] = weighted_sum(
                [-spectral_weight(n - m, instances) for m in range(here)], values
            )
        return carry

    lax.fori_loop(0, count_v, own_source, 0)

    pl.when((helps[0] | helps[1]) & (inst == 0))(functools.partial(pl.semaphore_wait, cross, 1))

    def pass_on(piece):
        aside_copies[piece].wait_recv()
        onward_copies[piece].start()

    for piece in range(ASIDE):
        pl.when(helps[piece])(functools.partial(pass_on, piece))
    for copy in always[len(always) - HELD :]:
        copy.start()
    for copy in moved:
        pl.when(jnp.logical_not(first))(copy.start)
    for step in (-1, -2):
        pl.when(above[step])(functools.partial(answered, step))
    two_back = rim_copies[STEPS.index(2)]
    two_ahead = rim_copies[STEPS.index(-2)]
    two_back.wait_recv()
    two_ahead.wait_recv()
    pl.when(shares)(shared_copy.start)
    for step in (1, -1):
        rim_copies[STEPS.index(step)].wait_recv()
    for face in range(2):
        picked = rims[picks[face]]
        amount = columns - shifts[face]
        for v in range(count_v):
            ghosts[face, v] = pltpu.roll(picked[v], amount, 1)

    extent = row_count + 8
    position = lax.broadcasted_iota(jnp.int32, (extent, columns), 0)
    first_beyond = position == my_rows
    second_beyond = position == my_rows + 1
    last_row = lax.broadcasted_iota(jnp.int32, (8, columns), 0) == 7

    def spatial(n, carry):
        fields = []
        for v in range(count_v):
            low = [ghosts[0, v, pl.ds(2 * n + layer, 1), :] for layer in range(2)]
            top = [ghosts[1, v, pl.ds(2 * n + layer, 1), :] for layer in range(2)]
            before = jnp.where(last_row, low[0], low[1])
            block_rows = jnp.concatenate([near[n, v], before], axis=0)
            fields.append(
                jnp.where(first_beyond, top[0], jnp.where(second_beyond, top[1], block_rows))
            )
        inverse = 1.0 / fields[0]
        squares = fields[1] * fields[1] + fields[2] * fields[2] + fields[3] * fields[3]
        pressure = GAMMA_MINUS * (fields[4] - 0.5 * squares * inverse)
        for v, flux in enumerate(flux_parts(fields, pressure, inverse, 1)):
            out[n, v] += differences(flux, fields[v], 0)[:row_count]
        fields = [field[:row_count] for field in fields]
        pressure = pressure[:row_count]
        inverse = inverse[:row_count]
        for v, flux in enumerate(flux_parts(fields, pressure, inverse, 2)):
            out[n, v] += differences(flux, fields[v], 1)
        return carry

    lax.fori_loop(0, here, spatial, 0)

    inside = lax.broadcasted_iota(jnp.int32, (row_count, columns), 0) < my_rows
    for v in range(count_v):
        for copy in far_copies[v * here : (v + 1) * here]:
            copy.wait_recv()
        values = [far[m, v] for m in range(here)]
        for n in range(here):
            source = weighted_sum(
                [spectral_weight(n - m - here, instances) for m in range(here)], values
            )
            out[n, v] = jnp.where(inside, out[n, v] - source, 0.0)
    for copy in always:
        copy.wait_send()
    for step, copy in zip(STEPS, rim_copies):
        pl.when(whole[step])(copy.wait_send)
    pl.when(shares)(shared_copy.wait_send)
    for piece in range(ASIDE):
        pl.when(first)(aside_copies[piece].wait_send)
        pl.when(helps[piece])(onward_copies[piece].wait_send)
        pl.when(jnp.logical_not(first))(moved[piece].wait_send)


def on_device(state, slot_of, conn_block, conn_side, conn_shift, rows):
    here, count_v, _, row_count, columns = state.shape
    instances = here * lax.axis_size("inst")
    blocks = slot_of.shape[0]
    whole = (here, count_v, row_count, columns)
    result = pl.pallas_call(
        functools.partial(kernel, instances),
        out_shape=jax.ShapeDtypeStruct(whole, jnp.float32),
        in_specs=[pl.BlockSpec(memory_space=pl.ANY)] * 6,
        out_specs=pl.BlockSpec(memory_space=pltpu.VMEM),
        scratch_shapes=[
            pltpu.VMEM(whole, jnp.float32),
            pltpu.VMEM(whole, jnp.float32),
            pltpu.VMEM((2 * (2 * REACH + 1), count_v, 2 * here, columns), jnp.float32),
            pltpu.VMEM((2, count_v, 2 * here, columns), jnp.float32),
            pltpu.VMEM((1, blocks), jnp.int32),
            pltpu.VMEM((2, blocks), jnp.int32),
            pltpu.VMEM((2, blocks), jnp.int32),
            pltpu.VMEM((2, blocks), jnp.int32),
            pltpu.VMEM((1, blocks), jnp.int32),
            pltpu.SemaphoreType.DMA((6,)),
            pltpu.SemaphoreType.DMA((here, count_v)),
            pltpu.SemaphoreType.DMA((here, count_v)),
            pltpu.SemaphoreType.DMA((2 * REACH + 1,)),
            pltpu.SemaphoreType.DMA((2 * REACH + 1,)),
            pltpu.VMEM((ASIDE, row_count, columns), jnp.float32),
            pltpu.SemaphoreType.DMA((3, ASIDE)),
            pltpu.SemaphoreType.REGULAR((4,)),
            pltpu.SemaphoreType.REGULAR,
            pltpu.SemaphoreType.REGULAR,
            pltpu.SemaphoreType.DMA,
        ],
        compiler_params=pltpu.CompilerParams(
            collective_id=0, has_side_effects=True, vmem_limit_bytes=16 * 2**20
        ),
        name="residual",
    )(
        *[
            pltpu.with_memory_space_constraint(operand, pltpu.HBM)
            for operand in (
                state.reshape(whole),
                slot_of.reshape(1, blocks),
                conn_block.T,
                conn_side.T,
                conn_shift.T,
                rows.reshape(1, blocks),
            )
        ]
    )
    return result.reshape(state.shape)


def solution(mesh):
    in_specs = (P("inst", None, "blk", None, None), P(), P(), P(), P(), P())
    out_specs = P("inst", None, "blk", None, None)
    return jax.shard_map(
        on_device, mesh=mesh, in_specs=in_specs, out_specs=out_specs, check_vma=False
    )
```

```python
import functools
import math

import jax
import jax.numpy as jnp
from jax import lax
from jax.experimental import pallas as pl
from jax.experimental.pallas import tpu as pltpu
from jax.sharding import PartitionSpec as P

REACH = 2
GAMMA_MINUS = 0.4
DAMPING = 0.05
FREQUENCY = 1.0
MESH = pl.DeviceIdType.MESH
OWN = REACH
STEPS = (-2, 2, -1, 1)
EARLY = 9
HELD = 5
ASIDE = 2
FIRST_ROW = 8


def spectral_weight(offset, count):
    offset %= count
    if offset == 0:
        return 0.0
    return 0.5 * FREQUENCY * (-1.0) ** offset / math.tan(math.pi * offset / count)


def weighted_sum(weights, values):
    total = None
    for weight, value in zip(weights, values):
        if weight == 0.0:
            continue
        term = weight * value
        total = term if total is None else total + term
    return total


def differences(flux, fields, axis):
    size = fields.shape[axis]
    wide = flux * (8.0 / 12.0)
    narrow = flux * (1.0 / 12.0)
    near = fields * (4.0 * DAMPING)
    far = fields * DAMPING
    ahead = (near - wide) + pltpu.roll(narrow - far, size - 1, axis)
    behind = (near + wide) - pltpu.roll(narrow + far, 1, axis)
    return (
        pltpu.roll(ahead, size - 1, axis)
        + pltpu.roll(behind, 1, axis)
        - fields * (6.0 * DAMPING)
    )


def flux_parts(fields, pressure, inverse, direction):
    velocity = fields[direction] * inverse
    parts = [
        fields[direction],
        fields[1] * velocity,
        fields[2] * velocity,
        fields[3] * velocity,
        (fields[4] + pressure) * velocity,
    ]
    parts[direction] = parts[direction] + pressure
    return parts


def kernel(
    instances, x_hbm, slot_hbm, block_hbm, side_hbm, shift_hbm, rows_hbm, out,
    near, far, rims, ghosts, slot, block, side, shift, rows,
    in_sems, far_send, far_recv, rim_send, rim_recv, hop, hop_sems, ack, cross, helper, share_sem,
):
    here, count_v, row_count, columns = near.shape
    inst = lax.axis_index("inst")
    me = lax.axis_index("blk")
    span = lax.axis_size("blk")
    partner = (1 - inst, me)
    place = lax.rem(me // 2, 4)

    def at(step):
        return (inst, lax.rem(me + step + span, span))

    rest = me >= FIRST_ROW
    first = rest & (place == 0)
    helps = [rest & (place == piece + 1) for piece in range(ASIDE)]
    beside = [
        lax.rem(me + (2 + 2 * piece) * jnp.where(place == 0, 1, -1) + span, span)
        for piece in range(ASIDE)
    ]

    def signal(semaphore, device):
        pl.semaphore_signal(semaphore, inc=1, device_id=device, device_id_type=MESH)

    def order(index):
        return jnp.where(index == 0, 5, 2 * index)

    below = {step: order(lax.rem(me + step + span, span)) < order(me) for step in STEPS}
    above = {step: jnp.logical_not(below[step]) for step in STEPS}
    barrier = pltpu.get_barrier_semaphore()
    signal(barrier, partner)
    for step in STEPS:
        pl.when(above[step])(functools.partial(signal, barrier, at(step)))
    greetings = 1 + jnp.where(helps[1], 1, 0)
    pl.when(first)(functools.partial(signal, barrier, (inst, beside[1])))
    for piece in range(ASIDE):
        takes_part = first | helps[piece]
        greetings = greetings + inst * jnp.where(takes_part, 1, 0)
        pl.when((inst == 0) & takes_part)(
            functools.partial(signal, barrier, (1 - inst, beside[piece]))
        )
    for step in STEPS:
        greetings = greetings + jnp.where(below[step], 1, 0)

    local = [
        pltpu.make_async_copy(source, target, in_sems.at[index])
        for index, (source, target) in enumerate(
            [
                (slot_hbm, slot),
                (rows_hbm, rows),
                (block_hbm, block),
                (side_hbm, side),
                (shift_hbm, shift),
                (x_hbm, near),
            ]
        )
    ]
    pl.semaphore_wait(barrier, greetings)

    far_copies = [
        pltpu.make_async_remote_copy(
            src_ref=x_hbm.at[m, v],
            dst_ref=far.at[m, v],
            send_sem=far_send.at[m, v],
            recv_sem=far_recv.at[m, v],
            device_id=partner,
            device_id_type=MESH,
        )
        for v in range(count_v)
        for m in range(here)
    ]
    always = far_copies[: len(far_copies) - ASIDE]
    moved = far_copies[: len(always) - 1 : -1]
    aside_copies = []
    onward_copies = []
    for piece in range(ASIDE):
        v, m = divmod(len(far_copies) - 1 - piece, here)
        aside_copies.append(
            pltpu.make_async_remote_copy(
                src_ref=x_hbm.at[m, v],
                dst_ref=hop.at[piece],
                send_sem=hop_sems.at[0, piece],
                recv_sem=hop_sems.at[1, piece],
                device_id=(inst, beside[piece]),
                device_id_type=MESH,
            )
        )
        onward_copies.append(
            pltpu.make_async_remote_copy(
                src_ref=hop.at[piece],
                dst_ref=far.at[m, v],
                send_sem=hop_sems.at[2, piece],
                recv_sem=far_recv.at[m, v],
                device_id=(1 - inst, beside[piece]),
                device_id_type=MESH,
            )
        )
    for copy in always[:EARLY]:
        copy.start()
    for copy in local:
        copy.start()
    for step in STEPS:
        pl.when(below[step])(functools.partial(signal, ack.at[STEPS.index(-step)], at(step)))
    pl.when(helps[1])(functools.partial(signal, helper, (inst, beside[1])))
    for piece in range(ASIDE):
        pl.when((inst == 1) & first)(functools.partial(signal, cross, (1 - inst, beside[piece])))

    for copy in local:
        copy.wait()
    slots = slot[...]
    numbers = lax.broadcasted_iota(jnp.int32, slots.shape, 1)
    mine = slots == me

    def looked_up(mask, values):
        return jnp.sum(jnp.where(mask, values, 0))

    my_rows = looked_up(mine, rows[...])
    picks = []
    shifts = []
    for face in range(2):
        neighbour = looked_up(mine, block[face : face + 1, :])
        neighbour_slot = looked_up(numbers == neighbour, slots)
        distance = lax.rem(neighbour_slot - me + (REACH + span), span)
        picks.append(
            jnp.clip(
                2 * distance + looked_up(mine, side[face : face + 1, :]), 0, rims.shape[0] - 1
            )
        )
        shifts.append(looked_up(mine, shift[face : face + 1, :]))

    high = [jnp.clip(my_rows - 1 - layer, 0, row_count - 1) for layer in range(2)]

    def gather_rim(v, carry):
        for n in range(here):
            rims[2 * OWN, v, 2 * n : 2 * n + 2, :] = near[n, v, 0:2, :]
            for layer in range(2):
                rims[2 * OWN + 1, v, 2 * n + layer : 2 * n + layer + 1, :] = near[
                    n, v, pl.ds(high[layer], 1), :
                ]
        return carry

    lax.fori_loop(0, count_v, gather_rim, 0)

    rim_copies = [
        pltpu.make_async_remote_copy(
            src_ref=rims.at[2 * OWN : 2 * OWN + 2],
            dst_ref=rims.at[2 * (OWN - step) : 2 * (OWN - step) + 2],
            send_sem=rim_send.at[OWN - step],
            recv_sem=rim_recv.at[OWN - step],
            device_id=at(step),
            device_id_type=MESH,
        )
        for step in STEPS
    ]
    core = lax.rem(me, 2)
    whole = {step: place >= 0 for step in STEPS}
    whole[1] = jnp.logical_not((place == 3) & (core == 1))
    whole[-1] = jnp.logical_not((place == 0) & (core == 0))
    shares = ((place == 0) & (core == 1)) | ((place == 3) & (core == 0))
    shared_copy = pltpu.make_async_remote_copy(
        src_ref=rims.at[pl.ds(8 * (1 - core), 2)],
        dst_ref=rims.at[pl.ds(6 - 4 * core, 2)],
        send_sem=share_sem,
        recv_sem=rim_recv.at[3 - 2 * core],
        device_id=(inst, me + 1 - 2 * core),
        device_id_type=MESH,
    )

    def answered(step):
        pl.semaphore_wait(ack.at[STEPS.index(step)], 1)
        pl.when(whole[step])(rim_copies[STEPS.index(step)].start)

    for step, copy in zip(STEPS, rim_copies):
        pl.when(below[step] & whole[step])(copy.start)
    for step in (1, 2):
        pl.when(above[step])(functools.partial(answered, step))

    @pl.when(first)
    def _():
        pl.semaphore_wait(helper, 1)
        for copy in aside_copies:
            copy.start()

    for copy in always[EARLY : len(always) - HELD]:
        copy.start()

    def own_source(v, carry):
        values = [near[m, v] for m in range(here)]
        for n in range(here):
            out[n, v] = weighted_sum(
                [-spectral_weight(n - m, instances) for m in range(here)], values
            )
        return carry

    lax.fori_loop(0, count_v, own_source, 0)

    pl.when((helps[0] | helps[1]) & (inst == 0))(functools.partial(pl.semaphore_wait, cross, 1))

    def pass_on(piece):
        aside_copies[piece].wait_recv()
        onward_copies[piece].start()

    for piece in range(ASIDE):
        pl.when(helps[piece])(functools.partial(pass_on, piece))
    for copy in always[len(always) - HELD :]:
        copy.start()
    for copy in moved:
        pl.when(jnp.logical_not(first))(copy.start)
    for step in (-1, -2):
        pl.when(above[step])(functools.partial(answered, step))
    two_back = rim_copies[STEPS.index(2)]
    two_ahead = rim_copies[STEPS.index(-2)]
    two_back.wait_recv()
    two_ahead.wait_recv()
    pl.when(shares)(shared_copy.start)
    for step in (1, -1):
        rim_copies[STEPS.index(step)].wait_recv()
    for face in range(2):
        picked = rims[picks[face]]
        amount = columns - shifts[face]
        for v in range(count_v):
            ghosts[face, v] = pltpu.roll(picked[v], amount, 1)

    extent = row_count + 8
    position = lax.broadcasted_iota(jnp.int32, (extent, columns), 0)
    first_beyond = position == my_rows
    second_beyond = position == my_rows + 1
    last_row = lax.broadcasted_iota(jnp.int32, (8, columns), 0) == 7

    def spatial(n, carry):
        fields = []
        for v in range(count_v):
            low = [ghosts[0, v, pl.ds(2 * n + layer, 1), :] for layer in range(2)]
            top = [ghosts[1, v, pl.ds(2 * n + layer, 1), :] for layer in range(2)]
            before = jnp.where(last_row, low[0], low[1])
            block_rows = jnp.concatenate([near[n, v], before], axis=0)
            fields.append(
                jnp.where(first_beyond, top[0], jnp.where(second_beyond, top[1], block_rows))
            )
        inverse = 1.0 / fields[0]
        squares = fields[1] * fields[1] + fields[2] * fields[2] + fields[3] * fields[3]
        pressure = GAMMA_MINUS * (fields[4] - 0.5 * squares * inverse)
        for v, flux in enumerate(flux_parts(fields, pressure, inverse, 1)):
            out[n, v] += differences(flux, fields[v], 0)[:row_count]
        fields = [field[:row_count] for field in fields]
        pressure = pressure[:row_count]
        inverse = inverse[:row_count]
        for v, flux in enumerate(flux_parts(fields, pressure, inverse, 2)):
            out[n, v] += differences(flux, fields[v], 1)
        return carry

    lax.fori_loop(0, here, spatial, 0)

    inside = lax.broadcasted_iota(jnp.int32, (row_count, columns), 0) < my_rows
    for v in range(count_v):
        for copy in far_copies[v * here : (v + 1) * here]:
            copy.wait_recv()
        values = [far[m, v] for m in range(here)]
        for n in range(here):
            source = weighted_sum(
                [spectral_weight(n - m - here, instances) for m in range(here)], values
            )
            out[n, v] = jnp.where(inside, out[n, v] - source, 0.0)
    for copy in always:
        copy.wait_send()
    for step, copy in zip(STEPS, rim_copies):
        pl.when(whole[step])(copy.wait_send)
    pl.when(shares)(shared_copy.wait_send)
    for piece in range(ASIDE):
        pl.when(first)(aside_copies[piece].wait_send)
        pl.when(helps[piece])(onward_copies[piece].wait_send)
        pl.when(jnp.logical_not(first))(moved[piece].wait_send)


def on_device(state, slot_of, conn_block, conn_side, conn_shift, rows):
    here, count_v, _, row_count, columns = state.shape
    instances = here * lax.axis_size("inst")
    blocks = slot_of.shape[0]
    whole = (here, count_v, row_count, columns)
    result = pl.pallas_call(
        functools.partial(kernel, instances),
        out_shape=jax.ShapeDtypeStruct(whole, jnp.float32),
        in_specs=[pl.BlockSpec(memory_space=pl.ANY)] * 6,
        out_specs=pl.BlockSpec(memory_space=pltpu.VMEM),
        scratch_shapes=[
            pltpu.VMEM(whole, jnp.float32),
            pltpu.VMEM(whole, jnp.float32),
            pltpu.VMEM((2 * (2 * REACH + 1), count_v, 2 * here, columns), jnp.float32),
            pltpu.VMEM((2, count_v, 2 * here, columns), jnp.float32),
            pltpu.VMEM((1, blocks), jnp.int32),
            pltpu.VMEM((2, blocks), jnp.int32),
            pltpu.VMEM((2, blocks), jnp.int32),
            pltpu.VMEM((2, blocks), jnp.int32),
            pltpu.VMEM((1, blocks), jnp.int32),
            pltpu.SemaphoreType.DMA((6,)),
            pltpu.SemaphoreType.DMA((here, count_v)),
            pltpu.SemaphoreType.DMA((here, count_v)),
            pltpu.SemaphoreType.DMA((2 * REACH + 1,)),
            pltpu.SemaphoreType.DMA((2 * REACH + 1,)),
            pltpu.VMEM((ASIDE, row_count, columns), jnp.float32),
            pltpu.SemaphoreType.DMA((3, ASIDE)),
            pltpu.SemaphoreType.REGULAR((4,)),
            pltpu.SemaphoreType.REGULAR,
            pltpu.SemaphoreType.REGULAR,
            pltpu.SemaphoreType.DMA,
        ],
        compiler_params=pltpu.CompilerParams(
            collective_id=0, has_side_effects=True, vmem_limit_bytes=16 * 2**20
        ),
        name="residual",
    )(
        *[
            pltpu.with_memory_space_constraint(operand, pltpu.HBM)
            for operand in (
                state.reshape(whole),
                slot_of.reshape(1, blocks),
                conn_block.T,
                conn_side.T,
                conn_shift.T,
                rows.reshape(1, blocks),
            )
        ]
    )
    return result.reshape(state.shape)


def solution(mesh):
    in_specs = (P("inst", None, "blk", None, None), P(), P(), P(), P(), P())
    out_specs = P("inst", None, "blk", None, None)
    return jax.shard_map(
        on_device, mesh=mesh, in_specs=in_specs, out_specs=out_specs, check_vma=False
    )
```
